32 devices in a mesh: ka: 8 (over z, core), ba: 4 (over y, x).
Axes of the slice: x: 2, y: 2, z: 4, core: 2. Of those that a mesh axis runs over, the one named last changes fastest.
Arguments:
- orbitals: bfloat16 [8, 4, 2, 32768], P('ka', 'ba'), may hold values from -6 to 6
- kpoint_coords: int32 [8, 3], replicated, may hold values from 0 to 3
Outputs:
- exchange_field: float32 [8, 4, 2, 32768], P('ka', 'ba')
The draws below stay inside these ranges and needn't reach their ends.
All inputs are finite; a program needn't handle non-finite values.
Results may differ from the reference program's by a relative error of at most 0.0074.
Values may be sent and summed in bfloat16 or wider, within the bound.
No kernel may reach another device: no remote copies, remote signals or barrier semaphores. Data moves between devices by JAX's collectives and lax.ppermute only.
A program may use at most 64 MiB of HBM per device.

```python
import math
import jax
import jax.numpy as jnp
from jax import lax

GRID = 32
CELLS = 32768
BANDS_DEV = 1
BANDS = 4
KPTS = 8
SHIFT = 2
MATCHES = 2
N_BA = 4


def with_ends(drawn, own_key, least, largest):
    spot = [jax.random.randint(jax.random.fold_in(own_key, axis), (), 0, length) for axis, length in enumerate(drawn.shape)]
    widest = drawn.shape.index(max(drawn.shape))
    neighbour = spot[:widest] + [(spot[widest] + 1) % drawn.shape[widest]] + spot[widest + 1:]
    return drawn.at[tuple(spot)].set(least).at[tuple(neighbour)].set(largest)


def level_of(rng, dims, pieces, least, largest):
    level, own = 1.0, jax.random.fold_in(rng, 6)
    for position, blocks in pieces:
        heights = jnp.exp(jax.random.uniform(jax.random.fold_in(own, position), (blocks,), jnp.float32, least / len(pieces), largest / len(pieces)))
        level = level * jnp.repeat(heights, dims[position] // blocks).reshape([-1 if axis == position else 1 for axis in range(len(dims))])
    return level


def bell_draw(own_key, dims, width, bound, split=(), kind=jnp.bfloat16):
    array = width * jax.random.normal(own_key, dims, jnp.float32)
    if split:
        array = array * level_of(own_key, dims, split, -0.22, 0.18)
    return jnp.clip(array, -bound, bound).astype(kind)


def setup_inputs(seed: int = 0) -> dict:
    keys = jax.random.split(jax.random.key(seed), 3)
    return {
        "orbitals": bell_draw(keys[0], (KPTS, BANDS, 2, CELLS), 1.0, 6.0, ((0, 8), (1, 4))),
        "kpoint_coords": with_ends(jax.random.randint(keys[1], (KPTS, 3), 0, 4), jax.random.fold_in(keys[1], 1), 0, 3).astype(jnp.int32),
    }


def wave_tables(grid, sign):
    index = jnp.arange(grid, dtype=jnp.int32)
    phase = (index[:, None] * index[None, :]) % grid
    angle = phase.astype(jnp.float32) * (2.0 * math.pi / grid)
    cosine = jnp.cos(angle)
    sine = sign * jnp.sin(angle)
    table = jnp.stack([jnp.stack([cosine, sine]), jnp.stack([-sine, cosine])])
    return table.astype(jnp.bfloat16)


def one_pass(field, table, grid):
    count = field.shape[0]
    shaped = field.reshape(count, 2, grid * grid, grid).astype(jnp.float32)
    result = jnp.einsum("pcme,dcfe->pdfm", shaped, table.astype(jnp.float32))
    return result.reshape(count, 2, grid ** 3)


def transform(field, table, grid):
    first = one_pass(field, table, grid).astype(jnp.bfloat16)
    second = one_pass(first, table, grid).astype(jnp.bfloat16)
    return one_pass(second, table, grid)


def coulomb_kernel(offset, grid):
    index = jnp.arange(grid, dtype=jnp.int32)
    signed = jnp.where(index < grid // 2, index, index - grid).astype(jnp.float32)
    along_x = signed[:, None, None] + offset[0]
    along_y = signed[None, :, None] + offset[1]
    along_z = signed[None, None, :] + offset[2]
    square = along_x * along_x + along_y * along_y + along_z * along_z
    return ((32.0 / (grid ** 3)) / (square + 0.25)).reshape(grid ** 3)


def pair_density(former, latter):
    f_real = former[..., :, None, 0, :].astype(jnp.float32)
    f_imag = former[..., :, None, 1, :].astype(jnp.float32)
    l_real = latter[..., None, :, 0, :].astype(jnp.float32)
    l_imag = latter[..., None, :, 1, :].astype(jnp.float32)
    real = l_real * f_real + l_imag * f_imag
    imag = l_real * f_imag - l_imag * f_real
    return jnp.stack([real, imag], axis=-2).astype(jnp.bfloat16)


def coulomb_fields(former, latter, kernel, forward, inverse, grid):
    density = pair_density(former, latter)
    flat = density.reshape(-1, 2, grid ** 3)
    spectrum = transform(flat, forward, grid)
    screened = (spectrum * kernel).astype(jnp.bfloat16)
    return transform(screened, inverse, grid).reshape(density.shape)


def apply_fields(fields, latter):
    w_real = fields[..., 0, :]
    w_imag = fields[..., 1, :]
    l_real = latter[..., None, :, 0, :].astype(jnp.float32)
    l_imag = latter[..., None, :, 1, :].astype(jnp.float32)
    real = -jnp.sum(l_real * w_real - l_imag * w_imag, axis=-2)
    imag = -jnp.sum(l_real * w_imag + l_imag * w_real, axis=-2)
    return jnp.stack([real, imag], axis=-2)


def back_fields(fields, former):
    w_real = fields[..., 0, :]
    w_imag = fields[..., 1, :]
    f_real = former[..., :, None, 0, :].astype(jnp.float32)
    f_imag = former[..., :, None, 1, :].astype(jnp.float32)
    real = -jnp.sum(f_real * w_real + f_imag * w_imag, axis=-3)
    imag = -jnp.sum(f_imag * w_real - f_real * w_imag, axis=-3)
    return jnp.stack([real, imag], axis=-2)


def reference(orbitals, kpoint_coords):
    groups = N_BA
    cells = CELLS
    forward = wave_tables(GRID, 1.0)
    inverse = wave_tables(GRID, -1.0)
    coords = kpoint_coords.astype(jnp.float32)
    shaped = orbitals.reshape(KPTS, groups, BANDS_DEV, 2, cells)
    group_ids = jnp.arange(groups, dtype=jnp.int32)

    def visit(number, result):
        here = jnp.asarray(number).astype(jnp.int32)
        source = ((here - SHIFT) % KPTS).astype(jnp.int32)
        own = lax.dynamic_index_in_dim(shaped, here, 0, keepdims=False)
        far = lax.dynamic_index_in_dim(shaped, source, 0, keepdims=False)
        offset = (lax.dynamic_index_in_dim(coords, here, 0, keepdims=False)
                  - lax.dynamic_index_in_dim(coords, source, 0, keepdims=False)) / 4.0
        kernel = coulomb_kernel(offset, GRID)
        gain = jnp.zeros((groups, BANDS_DEV, 2, cells), jnp.float32)
        back = jnp.zeros((groups, BANDS_DEV, 2, cells), jnp.float32)
        for matching in range(MATCHES):
            partner_ids = jnp.bitwise_xor(group_ids, jnp.int32(1 << matching))
            partner = far[partner_ids]
            fields = coulomb_fields(own, partner, kernel, forward, inverse, GRID)
            gain = gain + apply_fields(fields, partner)
            rounded = lax.optimization_barrier(back_fields(fields, own).astype(jnp.bfloat16))
            back = back + rounded.astype(jnp.float32)[partner_ids]
        row_here = lax.dynamic_index_in_dim(result, here, 0, keepdims=False)
        result = lax.dynamic_update_index_in_dim(result, row_here + gain, here, 0)
        row_source = lax.dynamic_index_in_dim(result, source, 0, keepdims=False)
        return lax.dynamic_update_index_in_dim(result, row_source + back, source, 0)

    start = jnp.zeros((KPTS, groups, BANDS_DEV, 2, cells), jnp.float32)
    final = lax.fori_loop(0, KPTS, visit, start)
    return final.reshape(KPTS, BANDS, 2, cells)
```

```python
import math

import numpy as np
import jax
import jax.numpy as jnp
from jax import lax
from jax.experimental import pallas as pl
from jax.experimental.pallas import tpu as pltpu
from jax.sharding import PartitionSpec as P

LANES = 128


class Layout:
    def __init__(self, cells):
        self.grid = round(cells ** (1.0 / 3.0))
        self.low = LANES // self.grid
        self.high = self.grid // self.low
        self.rows = self.grid * self.high


def roots(exponents, grid):
    angle = (exponents % grid).astype(np.float64) * (2.0 * math.pi / grid)
    return np.cos(angle).astype(np.float32), np.sin(angle).astype(np.float32)


def tables(lay):
    grid, low, high = lay.grid, lay.low, lay.high
    row = np.arange(lay.rows)
    lane = np.arange(LANES)
    fx, f0 = row // high, row % high
    f1, fz = lane // grid, lane % grid
    cos, sin = roots(np.outer(fx, fx) + low * np.outer(f0, f0), grid)
    rows_table = np.concatenate([cos, sin], axis=0)
    tw_cos, tw_sin = roots(np.outer(f0, f1), grid)
    cos, sin = roots(high * np.outer(f1, f1) + np.outer(fz, fz), grid)
    forward = np.block([[cos, -sin], [sin, cos]])
    inverse = np.block([[cos, sin], [-sin, cos]])
    narrow = [jnp.asarray(t, jnp.bfloat16) for t in (rows_table, forward, inverse)]
    return narrow + [jnp.asarray(np.concatenate([tw_cos, tw_sin], axis=0))]


def coulomb_kernel(offset, lay):
    grid, high = lay.grid, lay.high
    shape = (lay.rows, LANES)
    row = lax.broadcasted_iota(jnp.int32, shape, 0)
    lane = lax.broadcasted_iota(jnp.int32, shape, 1)

    def signed(index):
        return jnp.where(index < grid // 2, index, index - grid).astype(jnp.float32)

    along_x = signed(row // high) + offset[0]
    along_y = signed(lane // grid * high + row % high) + offset[1]
    along_z = signed(lane % grid) + offset[2]
    square = along_x * along_x + along_y * along_y + along_z * along_z
    return 32.0 / grid**3 / (square + 0.25)


def interleaved(field, lay):
    return field.reshape(2, lay.rows, LANES).transpose(1, 0, 2).reshape(2 * lay.rows, LANES)


def split_parts(ref, scratch, rows):
    scratch[...] = ref[...].astype(jnp.float32)
    return scratch[pl.ds(0, rows, 2), :], scratch[pl.ds(1, rows, 2), :]


def exchange_kernel(rows, matches, *refs):
    source_ref, refs = refs[0], refs[1:]
    target_refs, refs = refs[:matches], refs[matches:]
    coulomb_ref, rows_ref, forward_ref, inverse_ref, twiddle_ref = refs[:5]
    own_refs, return_ref = refs[5 : 5 + matches], refs[5 + matches]
    scratch = refs[6 + matches :]
    f32, bf16 = jnp.float32, jnp.bfloat16

    def dot(a, b):
        return jnp.dot(a, b, preferred_element_type=f32)

    s_real, s_imag = split_parts(source_ref, scratch[0], rows)
    targets = [split_parts(target_refs[j], scratch[1 + j], rows) for j in range(matches)]
    coulomb = coulomb_ref[...]
    coulomb = jnp.concatenate([coulomb, coulomb], axis=1)
    tw_cos, tw_sin = twiddle_ref[:rows], twiddle_ref[rows:]

    stage = []
    for t_real, t_imag in targets:
        real = s_real * t_real + s_imag * t_imag
        imag = s_real * t_imag - s_imag * t_real
        stage.append(jnp.concatenate([real.astype(bf16), imag.astype(bf16)], axis=1))
    stage = [dot(rows_ref[...], pair) for pair in stage]
    after = []
    for both in stage:
        real = both[:rows, :LANES] + both[rows:, LANES:]
        imag = both[:rows, LANES:] - both[rows:, :LANES]
        turned_real = real * tw_cos + imag * tw_sin
        turned_imag = imag * tw_cos - real * tw_sin
        after.append(jnp.concatenate([turned_real.astype(bf16), turned_imag.astype(bf16)], axis=1))
    stage = [dot(field, forward_ref[...]) for field in after]
    stage = [(field * coulomb).astype(bf16) for field in stage]
    stage = [dot(field, inverse_ref[...]) for field in stage]
    after = []
    for both in stage:
        real, imag = both[:, :LANES], both[:, LANES:]
        turned_real = real * tw_cos - imag * tw_sin
        turned_imag = imag * tw_cos + real * tw_sin
        after.append(jnp.concatenate([turned_real.astype(bf16), turned_imag.astype(bf16)], axis=1))
    stage = [dot(rows_ref[...], field) for field in after]
    total_real, total_imag = None, None
    for j, both in enumerate(stage):
        v_real = both[:rows, :LANES] - both[rows:, LANES:]
        v_imag = both[:rows, LANES:] + both[rows:, :LANES]
        t_real, t_imag = targets[j]
        own_refs[j][:rows] = (s_imag * v_imag - s_real * v_real).astype(bf16)
        own_refs[j][rows:] = (-(s_real * v_imag + s_imag * v_real)).astype(bf16)
        real = -(t_real * v_real + t_imag * v_imag)
        imag = t_real * v_imag - t_imag * v_real
        total_real = real if total_real is None else total_real + real
        total_imag = imag if total_imag is None else total_imag + imag
    return_ref[:rows] = total_real.astype(bf16)
    return_ref[rows:] = total_imag.astype(bf16)


def sum_kernel(rows, *refs):
    out_ref = refs[-1]
    total = refs[0][...].astype(jnp.float32)
    for ref in refs[1:-1]:
        total = total + ref[...].astype(jnp.float32)
    out_ref[pl.ds(0, rows, 2), :] = total[:rows]
    out_ref[pl.ds(1, rows, 2), :] = total[rows:]


def in_vmem(count):
    return [pl.BlockSpec(memory_space=pltpu.VMEM)] * count


def per_device(orbitals, kpoint_coords):
    own = orbitals[0, 0]
    cells = own.shape[-1]
    lay = Layout(cells)
    rows = lay.rows
    kpoints, groups = lax.axis_size("ka"), lax.axis_size("ba")
    steps = kpoints // 4
    matches = min(3, groups // 4 + 1)

    def shifted(value, by):
        return lax.ppermute(value, "ka", [(k, (k + by) % kpoints) for k in range(kpoints)])

    def partner(value, apart):
        return lax.ppermute(value, "ba", [(b, b ^ 2**apart) for b in range(groups)])

    source = shifted(own, steps)
    targets = [partner(own, j) for j in range(matches)]

    coords = kpoint_coords.astype(jnp.float32)
    here = lax.axis_index("ka")
    there = (here - steps) % kpoints
    offset = (coords[here] - coords[there]) / 4.0
    coulomb = coulomb_kernel(offset, lay)

    field = jax.ShapeDtypeStruct((2 * rows, LANES), jnp.bfloat16)
    outs = pl.pallas_call(
        lambda *refs: exchange_kernel(rows, matches, *refs),
        out_shape=[field] * (matches + 1),
        in_specs=in_vmem(matches + 6),
        out_specs=in_vmem(matches + 1),
        scratch_shapes=[pltpu.VMEM((2 * rows, LANES), jnp.float32)] * (matches + 1),
        compiler_params=pltpu.CompilerParams(vmem_limit_bytes=32 * 1024 * 1024),
        name="exchange",
    )(interleaved(source, lay), *[interleaved(t, lay) for t in targets], coulomb, *tables(lay))
    arrived = [shifted(outs[matches], -steps)]
    arrived += [partner(outs[j], j) for j in range(matches)]
    total = pl.pallas_call(
        lambda *refs: sum_kernel(rows, *refs),
        out_shape=jax.ShapeDtypeStruct((2 * rows, LANES), jnp.float32),
        in_specs=in_vmem(matches + 1),
        out_specs=in_vmem(1)[0],
        compiler_params=pltpu.CompilerParams(vmem_limit_bytes=32 * 1024 * 1024),
        name="total",
    )(*arrived)
    return total.reshape(rows, 2, LANES).transpose(1, 0, 2).reshape(1, 1, 2, cells)


def solution(mesh):
    return jax.shard_map(
        per_device,
        mesh=mesh,
        in_specs=(P("ka", "ba", None, None), P()),
        out_specs=P("ka", "ba", None, None),
        check_vma=False,
    )
```

```python
import math

import jax
import jax.numpy as jnp
from jax import lax
from jax.experimental import pallas as pl
from jax.experimental.pallas import tpu as pltpu
from jax.sharding import PartitionSpec as P

LANES = 128


class Layout:
    def __init__(self, cells):
        self.grid = round(cells ** (1.0 / 3.0))
        self.low = LANES // self.grid
        self.high = self.grid // self.low
        self.rows = self.grid * self.high


def cosine(steps, grid):
    folded = jnp.abs((steps & (grid - 1)) - grid // 2) - grid // 4
    angle = folded.astype(jnp.float32) * (2.0 * math.pi / grid)
    square = angle * angle
    series = jnp.zeros_like(angle)
    for order in range(13, 1, -2):
        series = (series + (-1) ** (order // 2) / math.factorial(order)) * square
    return angle + angle * series


def sine(steps, grid):
    return cosine(steps - grid // 4, grid)


def setup_kernel(lay, by, coords_ref, rows_ref, forward_ref, inverse_ref, twiddle_ref, coulomb_ref):
    grid, high, rows = lay.grid, lay.high, lay.rows
    column = lax.broadcasted_iota(jnp.int32, (rows, 1), 0)
    across = lax.broadcasted_iota(jnp.int32, (1, rows), 1)
    steps = (column // high) * (across // high) + lay.low * (column % high) * (across % high)
    rows_ref[:rows] = cosine(steps, grid).astype(jnp.bfloat16)
    rows_ref[rows:] = sine(steps, grid).astype(jnp.bfloat16)

    lane_row = lax.broadcasted_iota(jnp.int32, (LANES, 1), 0)
    lane = lax.broadcasted_iota(jnp.int32, (1, LANES), 1)
    steps = high * (lane_row // grid) * (lane // grid) + (lane_row % grid) * (lane % grid)
    cos = cosine(steps, grid).astype(jnp.bfloat16)
    sin = sine(steps, grid)
    minus = (-sin).astype(jnp.bfloat16)
    sin = sin.astype(jnp.bfloat16)
    for ref, lower, upper in ((forward_ref, sin, minus), (inverse_ref, minus, sin)):
        ref[:LANES, :LANES] = cos
        ref[LANES:, LANES:] = cos
        ref[LANES:, :LANES] = lower
        ref[:LANES, LANES:] = upper

    steps = (column % high) * (lane // grid)
    twiddle_ref[:rows] = cosine(steps, grid)
    twiddle_ref[rows:] = sine(steps, grid)

    kpoints = coords_ref.shape[1]
    here = lax.axis_index("ka")
    there = lax.rem(here + kpoints - by, kpoints)
    offset = [(coords_ref[d, here] - coords_ref[d, there]).astype(jnp.float32) / 4.0 for d in range(3)]

    def signed(index):
        return jnp.where(index < grid // 2, index, index - grid).astype(jnp.float32)

    along_x = signed(column // high) + offset[0]
    along_y = signed(lane // grid * high + column % high) + offset[1]
    along_z = signed(lane % grid) + offset[2]
    square = along_x * along_x + along_y * along_y + along_z * along_z
    coulomb_ref[...] = 32.0 / grid**3 / (square + 0.25)


def interleaved(field, lay):
    return field.reshape(2, lay.rows, LANES).transpose(1, 0, 2).reshape(2 * lay.rows, LANES)


def split_parts(ref, scratch, rows):
    scratch[...] = ref[...].astype(jnp.float32)
    return scratch[pl.ds(0, rows, 2), :], scratch[pl.ds(1, rows, 2), :]


def exchange_kernel(rows, matches, *refs):
    source_ref, refs = refs[0], refs[1:]
    target_refs, refs = refs[:matches], refs[matches:]
    rows_ref, forward_ref, inverse_ref, twiddle_ref, coulomb_ref = refs[:5]
    own_refs, return_ref = refs[5 : 5 + matches], refs[5 + matches]
    scratch = refs[6 + matches :]
    f32, bf16 = jnp.float32, jnp.bfloat16

    def dot(a, b):
        return jnp.dot(a, b, preferred_element_type=f32)

    s_real, s_imag = split_parts(source_ref, scratch[0], rows)
    targets = [split_parts(target_refs[j], scratch[1 + j], rows) for j in range(matches)]
    coulomb = coulomb_ref[...]
    coulomb = jnp.concatenate([coulomb, coulomb], axis=1)
    tw_cos, tw_sin = twiddle_ref[:rows], twiddle_ref[rows:]

    stage = []
    for t_real, t_imag in targets:
        real = s_real * t_real + s_imag * t_imag
        imag = s_real * t_imag - s_imag * t_real
        stage.append(jnp.concatenate([real.astype(bf16), imag.astype(bf16)], axis=1))
    stage = [dot(rows_ref[...], pair) for pair in stage]
    after = []
    for both in stage:
        real = both[:rows, :LANES] + both[rows:, LANES:]
        imag = both[:rows, LANES:] - both[rows:, :LANES]
        turned_real = real * tw_cos + imag * tw_sin
        turned_imag = imag * tw_cos - real * tw_sin
        after.append(jnp.concatenate([turned_real.astype(bf16), turned_imag.astype(bf16)], axis=1))
    stage = [dot(field, forward_ref[...]) for field in after]
    stage = [(field * coulomb).astype(bf16) for field in stage]
    stage = [dot(field, inverse_ref[...]) for field in stage]
    after = []
    for both in stage:
        real, imag = both[:, :LANES], both[:, LANES:]
        turned_real = real * tw_cos - imag * tw_sin
        turned_imag = imag * tw_cos + real * tw_sin
        after.append(jnp.concatenate([turned_real.astype(bf16), turned_imag.astype(bf16)], axis=1))
    stage = [dot(rows_ref[...], field) for field in after]
    total_real, total_imag = None, None
    for j, both in enumerate(stage):
        v_real = both[:rows, :LANES] - both[rows:, LANES:]
        v_imag = both[:rows, LANES:] + both[rows:, :LANES]
        t_real, t_imag = targets[j]
        own_refs[j][:rows] = (s_imag * v_imag - s_real * v_real).astype(bf16)
        own_refs[j][rows:] = (-(s_real * v_imag + s_imag * v_real)).astype(bf16)
        real = -(t_real * v_real + t_imag * v_imag)
        imag = t_real * v_imag - t_imag * v_real
        total_real = real if total_real is None else total_real + real
        total_imag = imag if total_imag is None else total_imag + imag
    return_ref[:rows] = total_real.astype(bf16)
    return_ref[rows:] = total_imag.astype(bf16)


def sum_kernel(rows, *refs):
    out_ref = refs[-1]
    total = refs[0][...].astype(jnp.float32)
    for ref in refs[1:-1]:
        total = total + ref[...].astype(jnp.float32)
    out_ref[pl.ds(0, rows, 2), :] = total[:rows]
    out_ref[pl.ds(1, rows, 2), :] = total[rows:]


def in_vmem(count):
    return [pl.BlockSpec(memory_space=pltpu.VMEM)] * count


def per_device(orbitals, kpoint_coords):
    own = orbitals[0, 0]
    cells = own.shape[-1]
    lay = Layout(cells)
    rows = lay.rows
    kpoints, groups = lax.axis_size("ka"), lax.axis_size("ba")
    steps = kpoints // 4
    matches = min(3, groups // 4 + 1)

    def shifted(value, by):
        return lax.ppermute(value, "ka", [(k, (k + by) % kpoints) for k in range(kpoints)])

    def partner(value, apart):
        return lax.ppermute(value, "ba", [(b, b ^ 2**apart) for b in range(groups)])

    source = shifted(own, steps)
    targets = [partner(own, j) for j in range(matches)]

    def shape(*dims, dtype=jnp.bfloat16):
        return jax.ShapeDtypeStruct(dims, dtype)

    limits = pltpu.CompilerParams(vmem_limit_bytes=32 * 1024 * 1024)
    tables = pl.pallas_call(
        lambda *refs: setup_kernel(lay, steps, *refs),
        out_shape=[
            shape(2 * rows, rows),
            shape(2 * LANES, 2 * LANES),
            shape(2 * LANES, 2 * LANES),
            shape(2 * rows, LANES, dtype=jnp.float32),
            shape(rows, LANES, dtype=jnp.float32),
        ],
        in_specs=[pl.BlockSpec(memory_space=pltpu.SMEM)],
        out_specs=in_vmem(5),
        compiler_params=limits,
        name="setup",
    )(kpoint_coords.T)

    outs = pl.pallas_call(
        lambda *refs: exchange_kernel(rows, matches, *refs),
        out_shape=[shape(2 * rows, LANES)] * (matches + 1),
        in_specs=in_vmem(matches + 6),
        out_specs=in_vmem(matches + 1),
        scratch_shapes=[pltpu.VMEM((2 * rows, LANES), jnp.float32)] * (matches + 1),
        compiler_params=limits,
        name="exchange",
    )(interleaved(source, lay), *[interleaved(t, lay) for t in targets], *tables)
    arrived = [shifted(outs[matches], -steps)]
    arrived += [partner(outs[j], j) for j in range(matches)]
    total = pl.pallas_call(
        lambda *refs: sum_kernel(rows, *refs),
        out_shape=shape(2 * rows, LANES, dtype=jnp.float32),
        in_specs=in_vmem(matches + 1),
        out_specs=in_vmem(1)[0],
        compiler_params=limits,
        name="total",
    )(*arrived)
    return total.reshape(rows, 2, LANES).transpose(1, 0, 2).reshape(1, 1, 2, cells)


def solution(mesh):
    return jax.shard_map(
        per_device,
        mesh=mesh,
        in_specs=(P("ka", "ba", None, None), P()),
        out_specs=P("ka", "ba", None, None),
        check_vma=False,
    )
```

```python
import math

import jax
import jax.numpy as jnp
from jax import lax
from jax.experimental import pallas as pl
from jax.experimental.pallas import tpu as pltpu
from jax.sharding import PartitionSpec as P

LANES = 128


class Layout:
    def __init__(self, cells):
        self.grid = round(cells ** (1.0 / 3.0))
        self.low = LANES // self.grid
        self.high = self.grid // self.low
        self.rows = self.grid * self.high


def cosine(steps, grid):
    folded = jnp.abs((steps & (grid - 1)) - grid // 2) - grid // 4
    angle = folded.astype(jnp.float32) * (2.0 * math.pi / grid)
    square = angle * angle
    series = jnp.zeros_like(angle)
    for order in range(13, 1, -2):
        series = (series + (-1) ** (order // 2) / math.factorial(order)) * square
    return angle + angle * series


def sine(steps, grid):
    return cosine(steps - grid // 4, grid)


def setup_kernel(lay, by, coords_ref, rows_ref, forward_ref, inverse_ref, twiddle_ref, coulomb_ref):
    grid, high, rows = lay.grid, lay.high, lay.rows
    column = lax.broadcasted_iota(jnp.int32, (rows, 1), 0)
    across = lax.broadcasted_iota(jnp.int32, (1, rows), 1)
    steps = (column // high) * (across // high) + lay.low * (column % high) * (across % high)
    rows_ref[:rows] = cosine(steps, grid).astype(jnp.bfloat16)
    rows_ref[rows:] = sine(steps, grid).astype(jnp.bfloat16)

    lane_row = lax.broadcasted_iota(jnp.int32, (LANES, 1), 0)
    lane = lax.broadcasted_iota(jnp.int32, (1, LANES), 1)
    steps = high * (lane_row // grid) * (lane // grid) + (lane_row % grid) * (lane % grid)
    cos = cosine(steps, grid).astype(jnp.bfloat16)
    sin = sine(steps, grid)
    minus = (-sin).astype(jnp.bfloat16)
    sin = sin.astype(jnp.bfloat16)
    for ref, lower, upper in ((forward_ref, sin, minus), (inverse_ref, minus, sin)):
        ref[:LANES, :LANES] = cos
        ref[LANES:, LANES:] = cos
        ref[LANES:, :LANES] = lower
        ref[:LANES, LANES:] = upper

    steps = (column % high) * (lane // grid)
    twiddle_ref[:rows] = cosine(steps, grid)
    twiddle_ref[rows:] = sine(steps, grid)

    kpoints = coords_ref.shape[1]
    here = lax.axis_index("ka")
    there = lax.rem(here + kpoints - by, kpoints)
    offset = [(coords_ref[d, here] - coords_ref[d, there]).astype(jnp.float32) / 4.0 for d in range(3)]

    def signed(index):
        return jnp.where(index < grid // 2, index, index - grid).astype(jnp.float32)

    along_x = signed(column // high) + offset[0]
    along_y = signed(lane // grid * high + column % high) + offset[1]
    along_z = signed(lane % grid) + offset[2]
    square = along_x * along_x + along_y * along_y + along_z * along_z
    coulomb_ref[...] = 32.0 / grid**3 / (square + 0.25)


def interleaved(field, lay):
    return field.reshape(2, lay.rows, LANES).transpose(1, 0, 2).reshape(2 * lay.rows, LANES)


def split_parts(ref, scratch, rows):
    scratch[...] = ref[...].astype(jnp.float32)
    return scratch[pl.ds(0, rows, 2), :], scratch[pl.ds(1, rows, 2), :]


def exchange_kernel(rows, matches, *refs):
    target_refs, source_ref, refs = refs[:matches], refs[matches], refs[matches + 1 :]
    rows_ref, forward_ref, inverse_ref, twiddle_ref, coulomb_ref = refs[:5]
    own_refs, return_ref = refs[5 : 5 + matches], refs[5 + matches]
    scratch = refs[6 + matches :]
    f32, bf16 = jnp.float32, jnp.bfloat16

    def dot(a, b):
        return jnp.dot(a, b, preferred_element_type=f32)

    s_real, s_imag = split_parts(source_ref, scratch[0], rows)
    targets = [split_parts(target_refs[j], scratch[1 + j], rows) for j in range(matches)]
    coulomb = coulomb_ref[...]
    coulomb = jnp.concatenate([coulomb, coulomb], axis=1)
    tw_cos, tw_sin = twiddle_ref[:rows], twiddle_ref[rows:]

    stage = []
    for t_real, t_imag in targets:
        real = s_real * t_real + s_imag * t_imag
        imag = s_real * t_imag - s_imag * t_real
        stage.append(jnp.concatenate([real.astype(bf16), imag.astype(bf16)], axis=1))
    stage = [dot(rows_ref[...], pair) for pair in stage]
    after = []
    for both in stage:
        real = both[:rows, :LANES] + both[rows:, LANES:]
        imag = both[:rows, LANES:] - both[rows:, :LANES]
        turned_real = real * tw_cos + imag * tw_sin
        turned_imag = imag * tw_cos - real * tw_sin
        after.append(jnp.concatenate([turned_real.astype(bf16), turned_imag.astype(bf16)], axis=1))
    stage = [dot(field, forward_ref[...]) for field in after]
    stage = [(field * coulomb).astype(bf16) for field in stage]
    stage = [dot(field, inverse_ref[...]) for field in stage]
    after = []
    for both in stage:
        real, imag = both[:, :LANES], both[:, LANES:]
        turned_real = real * tw_cos - imag * tw_sin
        turned_imag = imag * tw_cos + real * tw_sin
        after.append(jnp.concatenate([turned_real.astype(bf16), turned_imag.astype(bf16)], axis=1))
    stage = [dot(rows_ref[...], field) for field in after]
    total_real, total_imag = None, None
    for j, both in enumerate(stage):
        v_real = both[:rows, :LANES] - both[rows:, LANES:]
        v_imag = both[:rows, LANES:] + both[rows:, :LANES]
        t_real, t_imag = targets[j]
        own_refs[j][:rows] = (s_imag * v_imag - s_real * v_real).astype(bf16)
        own_refs[j][rows:] = (-(s_real * v_imag + s_imag * v_real)).astype(bf16)
        real = -(t_real * v_real + t_imag * v_imag)
        imag = t_real * v_imag - t_imag * v_real
        total_real = real if total_real is None else total_real + real
        total_imag = imag if total_imag is None else total_imag + imag
    return_ref[:rows] = total_real.astype(bf16)
    return_ref[rows:] = total_imag.astype(bf16)


def sum_kernel(rows, *refs):
    out_ref = refs[-1]
    total = refs[0][...].astype(jnp.float32)
    for ref in refs[1:-1]:
        total = total + ref[...].astype(jnp.float32)
    out_ref[pl.ds(0, rows, 2), :] = total[:rows]
    out_ref[pl.ds(1, rows, 2), :] = total[rows:]


def in_vmem(count):
    return [pl.BlockSpec(memory_space=pltpu.VMEM)] * count


def per_device(orbitals, kpoint_coords):
    own = orbitals[0, 0]
    cells = own.shape[-1]
    lay = Layout(cells)
    rows = lay.rows
    kpoints, groups = lax.axis_size("ka"), lax.axis_size("ba")
    steps = kpoints // 4
    matches = min(3, groups // 4 + 1)

    def shifted(value, by):
        return lax.ppermute(value, "ka", [(k, (k + by) % kpoints) for k in range(kpoints)])

    def partner(value, apart):
        return lax.ppermute(value, "ba", [(b, b ^ 2**apart) for b in range(groups)])

    source = shifted(own, steps)
    targets = [partner(own, j) for j in range(matches)]

    def shape(*dims, dtype=jnp.bfloat16):
        return jax.ShapeDtypeStruct(dims, dtype)

    limits = pltpu.CompilerParams(vmem_limit_bytes=32 * 1024 * 1024)
    tables = pl.pallas_call(
        lambda *refs: setup_kernel(lay, steps, *refs),
        out_shape=[
            shape(2 * rows, rows),
            shape(2 * LANES, 2 * LANES),
            shape(2 * LANES, 2 * LANES),
            shape(2 * rows, LANES, dtype=jnp.float32),
            shape(rows, LANES, dtype=jnp.float32),
        ],
        in_specs=[pl.BlockSpec(memory_space=pltpu.SMEM)],
        out_specs=in_vmem(5),
        compiler_params=limits,
        name="setup",
    )(kpoint_coords.T)

    outs = pl.pallas_call(
        lambda *refs: exchange_kernel(rows, matches, *refs),
        out_shape=[shape(2 * rows, LANES)] * (matches + 1),
        in_specs=in_vmem(matches + 6),
        out_specs=in_vmem(matches + 1),
        scratch_shapes=[pltpu.VMEM((2 * rows, LANES), jnp.float32)] * (matches + 1),
        compiler_params=limits,
        name="exchange",
    )(*[interleaved(t, lay) for t in targets], interleaved(source, lay), *tables)
    arrived = [partner(outs[j], j) for j in range(matches)]
    arrived += [shifted(outs[matches], -steps)]
    total = pl.pallas_call(
        lambda *refs: sum_kernel(rows, *refs),
        out_shape=shape(2 * rows, LANES, dtype=jnp.float32),
        in_specs=in_vmem(matches + 1),
        out_specs=in_vmem(1)[0],
        compiler_params=limits,
        name="total",
    )(*arrived)
    return total.reshape(rows, 2, LANES).transpose(1, 0, 2).reshape(1, 1, 2, cells)


def solution(mesh):
    return jax.shard_map(
        per_device,
        mesh=mesh,
        in_specs=(P("ka", "ba", None, None), P()),
        out_specs=P("ka", "ba", None, None),
        check_vma=False,
    )
```

```python
import math

import jax
import jax.numpy as jnp
from jax import lax
from jax.experimental import pallas as pl
from jax.experimental.pallas import tpu as pltpu
from jax.sharding import PartitionSpec as P

LANES = 128


class Layout:
    def __init__(self, cells):
        self.grid = round(cells ** (1.0 / 3.0))
        self.low = LANES // self.grid
        self.high = self.grid // self.low
        self.rows = self.grid * self.high


def cosine(steps, grid):
    folded = jnp.abs((steps & (grid - 1)) - grid // 2) - grid // 4
    angle = folded.astype(jnp.float32) * (2.0 * math.pi / grid)
    square = angle * angle
    series = jnp.zeros_like(angle)
    for order in range(13, 1, -2):
        series = (series + (-1) ** (order // 2) / math.factorial(order)) * square
    return angle + angle * series


def sine(steps, grid):
    return cosine(steps - grid // 4, grid)


def setup_kernel(lay, by, coords_ref, rows_ref, forward_ref, inverse_ref, twiddle_ref, coulomb_ref):
    grid, high, rows = lay.grid, lay.high, lay.rows
    column = lax.broadcasted_iota(jnp.int32, (rows, 1), 0)
    across = lax.broadcasted_iota(jnp.int32, (1, rows), 1)
    steps = (column // high) * (across // high) + lay.low * (column % high) * (across % high)
    rows_ref[:rows] = cosine(steps, grid).astype(jnp.bfloat16)
    rows_ref[rows:] = sine(steps, grid).astype(jnp.bfloat16)

    lane_row = lax.broadcasted_iota(jnp.int32, (LANES, 1), 0)
    lane = lax.broadcasted_iota(jnp.int32, (1, LANES), 1)
    steps = high * (lane_row // grid) * (lane // grid) + (lane_row % grid) * (lane % grid)
    cos = cosine(steps, grid).astype(jnp.bfloat16)
    sin = sine(steps, grid)
    minus = (-sin).astype(jnp.bfloat16)
    sin = sin.astype(jnp.bfloat16)
    for ref, lower, upper in ((forward_ref, sin, minus), (inverse_ref, minus, sin)):
        ref[:LANES, :LANES] = cos
        ref[LANES:, LANES:] = cos
        ref[LANES:, :LANES] = lower
        ref[:LANES, LANES:] = upper

    steps = (column % high) * (lane // grid)
    twiddle_ref[:rows] = cosine(steps, grid)
    twiddle_ref[rows:] = sine(steps, grid)

    kpoints = coords_ref.shape[1]
    here = lax.axis_index("ka")
    there = lax.rem(here + kpoints - by, kpoints)
    offset = [(coords_ref[d, here] - coords_ref[d, there]).astype(jnp.float32) / 4.0 for d in range(3)]

    def signed(index):
        return jnp.where(index < grid // 2, index, index - grid).astype(jnp.float32)

    along_x = signed(column // high) + offset[0]
    along_y = signed(lane // grid * high + column % high) + offset[1]
    along_z = signed(lane % grid) + offset[2]
    square = along_x * along_x + along_y * along_y + along_z * along_z
    coulomb_ref[...] = 32.0 / grid**3 / (square + 0.25)


def interleaved(field, lay):
    return field.reshape(2, lay.rows, LANES).transpose(1, 0, 2).reshape(2 * lay.rows, LANES)


def split_parts(ref, scratch, rows):
    scratch[...] = ref[...].astype(jnp.float32)
    return scratch[pl.ds(0, rows, 2), :], scratch[pl.ds(1, rows, 2), :]


def exchange_kernel(rows, matches, *refs):
    target_refs, source_ref, refs = refs[:matches], refs[matches], refs[matches + 1 :]
    rows_ref, forward_ref, inverse_ref, twiddle_ref, coulomb_ref = refs[:5]
    own_refs, return_ref = refs[5 : 5 + matches], refs[5 + matches]
    scratch = refs[6 + matches :]
    f32, bf16 = jnp.float32, jnp.bfloat16

    def dot(a, b):
        return jnp.dot(a, b, preferred_element_type=f32)

    s_real, s_imag = split_parts(source_ref, scratch[0], rows)
    targets = [split_parts(target_refs[j], scratch[1 + j], rows) for j in range(matches)]
    coulomb = coulomb_ref[...]
    coulomb = jnp.concatenate([coulomb, coulomb], axis=1)

    pairs = []
    for t_real, t_imag in targets:
        real = s_real * t_real + s_imag * t_imag
        imag = s_real * t_imag - s_imag * t_real
        pairs.append(jnp.concatenate([real.astype(bf16), imag.astype(bf16)], axis=1))

    def turned(real, imag, cos, sin):
        return jnp.concatenate([(real * cos + imag * sin).astype(bf16), (imag * cos - real * sin).astype(bf16)], axis=1)

    chunk = rows
    spans = [slice(at, at + chunk) for at in range(0, rows, chunk)]
    tables = []
    for span in spans:
        lower = slice(rows + span.start, rows + span.stop)
        tables.append((rows_ref[span], rows_ref[lower], twiddle_ref[span], twiddle_ref[lower]))

    fields = [[] for _ in pairs]
    for span, (row_cos, row_sin, tw_cos, tw_sin) in zip(spans, tables):
        both = [(dot(row_cos, pair), dot(row_sin, pair)) for pair in pairs]
        stage = [
            turned(c[:, :LANES] + s[:, LANES:], c[:, LANES:] - s[:, :LANES], tw_cos, tw_sin) for c, s in both
        ]
        stage = [dot(field, forward_ref[...]) for field in stage]
        stage = [(field * coulomb[span]).astype(bf16) for field in stage]
        stage = [dot(field, inverse_ref[...]) for field in stage]
        for j, field in enumerate(stage):
            fields[j].append(turned(field[:, :LANES], field[:, LANES:], tw_cos, -tw_sin))
    fields = [jnp.concatenate(parts, axis=0) for parts in fields]
    for span, (row_cos, row_sin, _, _) in zip(spans, tables):
        lower = slice(rows + span.start, rows + span.stop)
        total_real, total_imag = None, None
        for j, field in enumerate(fields):
            c, s = dot(row_cos, field), dot(row_sin, field)
            v_real = c[:, :LANES] - s[:, LANES:]
            v_imag = c[:, LANES:] + s[:, :LANES]
            (t_real, t_imag), a, b = targets[j], s_real[span], s_imag[span]
            t_real, t_imag = t_real[span], t_imag[span]
            own_refs[j][span] = (b * v_imag - a * v_real).astype(bf16)
            own_refs[j][lower] = (-(a * v_imag + b * v_real)).astype(bf16)
            real = t_real * v_real + t_imag * v_imag
            imag = t_real * v_imag - t_imag * v_real
            total_real = real if total_real is None else total_real + real
            total_imag = imag if total_imag is None else total_imag + imag
        return_ref[span] = (-total_real).astype(bf16)
        return_ref[lower] = total_imag.astype(bf16)


def sum_kernel(rows, *refs):
    out_ref = refs[-1]
    total = refs[0][...].astype(jnp.float32)
    for ref in refs[1:-1]:
        total = total + ref[...].astype(jnp.float32)
    out_ref[pl.ds(0, rows, 2), :] = total[:rows]
    out_ref[pl.ds(1, rows, 2), :] = total[rows:]


def in_vmem(count):
    return [pl.BlockSpec(memory_space=pltpu.VMEM)] * count


def per_device(orbitals, kpoint_coords):
    own = orbitals[0, 0]
    cells = own.shape[-1]
    lay = Layout(cells)
    rows = lay.rows
    kpoints, groups = lax.axis_size("ka"), lax.axis_size("ba")
    steps = kpoints // 4
    matches = min(3, groups // 4 + 1)

    def shifted(value, by):
        return lax.ppermute(value, "ka", [(k, (k + by) % kpoints) for k in range(kpoints)])

    def partner(value, apart):
        return lax.ppermute(value, "ba", [(b, b ^ 2**apart) for b in range(groups)])

    source = shifted(own, steps)
    targets = [partner(own, j) for j in range(matches)]

    def shape(*dims, dtype=jnp.bfloat16):
        return jax.ShapeDtypeStruct(dims, dtype)

    limits = pltpu.CompilerParams(vmem_limit_bytes=32 * 1024 * 1024)
    tables = pl.pallas_call(
        lambda *refs: setup_kernel(lay, steps, *refs),
        out_shape=[
            shape(2 * rows, rows),
            shape(2 * LANES, 2 * LANES),
            shape(2 * LANES, 2 * LANES),
            shape(2 * rows, LANES, dtype=jnp.float32),
            shape(rows, LANES, dtype=jnp.float32),
        ],
        in_specs=[pl.BlockSpec(memory_space=pltpu.SMEM)],
        out_specs=in_vmem(5),
        compiler_params=limits,
        name="setup",
    )(kpoint_coords.T)

    outs = pl.pallas_call(
        lambda *refs: exchange_kernel(rows, matches, *refs),
        out_shape=[shape(2 * rows, LANES)] * (matches + 1),
        in_specs=in_vmem(matches + 6),
        out_specs=in_vmem(matches + 1),
        scratch_shapes=[pltpu.VMEM((2 * rows, LANES), jnp.float32)] * (matches + 1),
        compiler_params=limits,
        name="exchange",
    )(*[interleaved(t, lay) for t in targets], interleaved(source, lay), *tables)
    arrived = [partner(outs[j], j) for j in range(matches)]
    arrived += [shifted(outs[matches], -steps)]
    total = pl.pallas_call(
        lambda *refs: sum_kernel(rows, *refs),
        out_shape=shape(2 * rows, LANES, dtype=jnp.float32),
        in_specs=in_vmem(matches + 1),
        out_specs=in_vmem(1)[0],
        compiler_params=limits,
        name="total",
    )(*arrived)
    return total.reshape(rows, 2, LANES).transpose(1, 0, 2).reshape(1, 1, 2, cells)


def solution(mesh):
    return jax.shard_map(
        per_device,
        mesh=mesh,
        in_specs=(P("ka", "ba", None, None), P()),
        out_specs=P("ka", "ba", None, None),
        check_vma=False,
    )
```

```python
import math

import jax
import jax.numpy as jnp
from jax import lax
from jax.experimental import pallas as pl
from jax.experimental.pallas import tpu as pltpu
from jax.sharding import PartitionSpec as P

LANES = 128


class Layout:
    def __init__(self, cells):
        self.grid = round(cells ** (1.0 / 3.0))
        self.low = LANES // self.grid
        self.high = self.grid // self.low
        self.rows = self.grid * self.high


def cosine(steps, grid):
    folded = jnp.abs((steps & (grid - 1)) - grid // 2) - grid // 4
    angle = folded.astype(jnp.float32) * (2.0 * math.pi / grid)
    square = angle * angle
    series = jnp.zeros_like(angle)
    for order in range(13, 1, -2):
        series = (series + (-1) ** (order // 2) / math.factorial(order)) * square
    return angle + angle * series


def sine(steps, grid):
    return cosine(steps - grid // 4, grid)


def setup_kernel(lay, by, coords_ref, rows_ref, forward_ref, inverse_ref, twiddle_ref, coulomb_ref):
    grid, high, rows = lay.grid, lay.high, lay.rows
    column = lax.broadcasted_iota(jnp.int32, (rows, 1), 0)
    across = lax.broadcasted_iota(jnp.int32, (1, rows), 1)
    steps = (column // high) * (across // high) + lay.low * (column % high) * (across % high)
    rows_ref[:rows] = cosine(steps, grid).astype(jnp.bfloat16)
    rows_ref[rows:] = sine(steps, grid).astype(jnp.bfloat16)

    lane_row = lax.broadcasted_iota(jnp.int32, (LANES, 1), 0)
    lane = lax.broadcasted_iota(jnp.int32, (1, LANES), 1)
    steps = high * (lane_row // grid) * (lane // grid) + (lane_row % grid) * (lane % grid)
    cos = cosine(steps, grid).astype(jnp.bfloat16)
    sin = sine(steps, grid)
    minus = (-sin).astype(jnp.bfloat16)
    sin = sin.astype(jnp.bfloat16)
    for ref, lower, upper in ((forward_ref, sin, minus), (inverse_ref, minus, sin)):
        ref[:LANES, :LANES] = cos
        ref[LANES:, LANES:] = cos
        ref[LANES:, :LANES] = lower
        ref[:LANES, LANES:] = upper

    steps = (column % high) * (lane // grid)
    twiddle_ref[:rows] = cosine(steps, grid)
    twiddle_ref[rows:] = sine(steps, grid)

    kpoints = coords_ref.shape[1]
    here = worker(lax.axis_index("ka"))
    there = lax.rem(here + kpoints - by, kpoints)
    offset = [(coords_ref[d, here] - coords_ref[d, there]).astype(jnp.float32) / 4.0 for d in range(3)]

    def signed(index):
        return jnp.where(index < grid // 2, index, index - grid).astype(jnp.float32)

    along_x = signed(column // high) + offset[0]
    along_y = signed(lane // grid * high + column % high) + offset[1]
    along_z = signed(lane % grid) + offset[2]
    square = along_x * along_x + along_y * along_y + along_z * along_z
    coulomb_ref[...] = 32.0 / grid**3 / (square + 0.25)


def interleaved(field, lay):
    return field.reshape(2, lay.rows, LANES).transpose(1, 0, 2).reshape(2 * lay.rows, LANES)


def worker(device):
    return device ^ 1


def split_parts(ref, scratch, rows):
    scratch[...] = ref[...].astype(jnp.float32)
    return scratch[pl.ds(0, rows, 2), :], scratch[pl.ds(1, rows, 2), :]


def exchange_kernel(rows, slots, *refs):
    matches = len(slots[0]) - 1
    target_refs, source_ref, refs = refs[:matches], refs[matches], refs[matches + 1 :]
    rows_ref, forward_ref, inverse_ref, twiddle_ref, coulomb_ref = refs[:5]
    out_refs, scratch = refs[5 : 6 + matches], refs[6 + matches :]
    odd = lax.rem(worker(lax.axis_index("ka")), 2) == 1
    f32, bf16 = jnp.float32, jnp.bfloat16

    def dot(a, b):
        return jnp.dot(a, b, preferred_element_type=f32)

    s_real, s_imag = split_parts(source_ref, scratch[0], rows)
    targets = [split_parts(target_refs[j], scratch[1 + j], rows) for j in range(matches)]
    coulomb = coulomb_ref[...]
    coulomb = jnp.concatenate([coulomb, coulomb], axis=1)

    pairs = []
    for t_real, t_imag in targets:
        real = s_real * t_real + s_imag * t_imag
        imag = s_real * t_imag - s_imag * t_real
        pairs.append(jnp.concatenate([real.astype(bf16), imag.astype(bf16)], axis=1))

    def turned(real, imag, cos, sin):
        return jnp.concatenate([(real * cos + imag * sin).astype(bf16), (imag * cos - real * sin).astype(bf16)], axis=1)

    row_cos, row_sin = rows_ref[:rows], rows_ref[rows:]
    tw_cos, tw_sin = twiddle_ref[:rows], twiddle_ref[rows:]
    both = [(dot(row_cos, pair), dot(row_sin, pair)) for pair in pairs]
    stage = [turned(c[:, :LANES] + s[:, LANES:], c[:, LANES:] - s[:, :LANES], tw_cos, tw_sin) for c, s in both]
    stage = [dot(field, forward_ref[...]) for field in stage]
    stage = [(field * coulomb).astype(bf16) for field in stage]
    stage = [dot(field, inverse_ref[...]) for field in stage]
    stage = [turned(field[:, :LANES], field[:, LANES:], tw_cos, -tw_sin) for field in stage]
    results = []
    total_real, total_imag = None, None
    for (t_real, t_imag), field in zip(targets, stage):
        c, s = dot(row_cos, field), dot(row_sin, field)
        v_real = c[:, :LANES] - s[:, LANES:]
        v_imag = c[:, LANES:] + s[:, :LANES]
        real = s_imag * v_imag - s_real * v_real
        imag = -(s_real * v_imag + s_imag * v_real)
        results.append((real.astype(bf16), imag.astype(bf16)))
        real = t_real * v_real + t_imag * v_imag
        imag = t_real * v_imag - t_imag * v_real
        total_real = real if total_real is None else total_real + real
        total_imag = imag if total_imag is None else total_imag + imag
    results.append(((-total_real).astype(bf16), total_imag.astype(bf16)))
    for out_ref, even_slot, odd_slot in zip(out_refs, *slots):
        for part, span in enumerate((slice(0, rows), slice(rows, 2 * rows))):
            value = results[even_slot][part]
            if even_slot != odd_slot:
                value = jnp.where(odd, results[odd_slot][part], value)
            out_ref[span] = value


def sum_kernel(rows, *refs):
    out_ref = refs[-1]
    total = refs[0][...].astype(jnp.float32)
    for ref in refs[1:-1]:
        total = total + ref[...].astype(jnp.float32)
    out_ref[pl.ds(0, rows, 2), :] = total[:rows]
    out_ref[pl.ds(1, rows, 2), :] = total[rows:]


def in_vmem(count):
    return [pl.BlockSpec(memory_space=pltpu.VMEM)] * count


def per_device(orbitals, kpoint_coords):
    own = orbitals[0, 0]
    cells = own.shape[-1]
    lay = Layout(cells)
    rows = lay.rows
    kpoints, groups = lax.axis_size("ka"), lax.axis_size("ba")
    steps = kpoints // 4
    matches = min(3, groups // 4 + 1)

    def moved(value, step, order, back):
        pairs = []
        for k in range(kpoints):
            for b in range(groups):
                part = order[k % 2][step]
                if part == matches:
                    home = (k - steps) % kpoints * groups + b
                else:
                    home = k * groups + (b ^ 2 ** ((part + k) % matches))
                away = worker(k) * groups + b
                pairs.append((away, home) if back else (home, away))
        return lax.ppermute(value, ("ka", "ba"), pairs)

    straight = list(range(matches + 1))
    arrivals = [moved(own, step, (straight, straight), False) for step in straight]
    slots = (straight[:matches][::-1] + straight[matches:], straight[matches:] + straight[:matches])

    def shape(*dims, dtype=jnp.bfloat16):
        return jax.ShapeDtypeStruct(dims, dtype)

    limits = pltpu.CompilerParams(vmem_limit_bytes=32 * 1024 * 1024)
    tables = pl.pallas_call(
        lambda *refs: setup_kernel(lay, steps, *refs),
        out_shape=[
            shape(2 * rows, rows),
            shape(2 * LANES, 2 * LANES),
            shape(2 * LANES, 2 * LANES),
            shape(2 * rows, LANES, dtype=jnp.float32),
            shape(rows, LANES, dtype=jnp.float32),
        ],
        in_specs=[pl.BlockSpec(memory_space=pltpu.SMEM)],
        out_specs=in_vmem(5),
        compiler_params=limits,
        name="setup",
    )(kpoint_coords.T)

    outs = pl.pallas_call(
        lambda *refs: exchange_kernel(rows, slots, *refs),
        out_shape=[shape(2 * rows, LANES)] * (matches + 1),
        in_specs=in_vmem(matches + 6),
        out_specs=in_vmem(matches + 1),
        scratch_shapes=[pltpu.VMEM((2 * rows, LANES), jnp.float32)] * (matches + 1),
        compiler_params=limits,
        name="exchange",
    )(*[interleaved(arrival, lay) for arrival in arrivals], *tables)
    returned = [moved(outs[step], step, slots, True) for step in straight]
    total = pl.pallas_call(
        lambda *refs: sum_kernel(rows, *refs),
        out_shape=shape(2 * rows, LANES, dtype=jnp.float32),
        in_specs=in_vmem(matches + 1),
        out_specs=in_vmem(1)[0],
        compiler_params=limits,
        name="total",
    )(*returned)
    return total.reshape(rows, 2, LANES).transpose(1, 0, 2).reshape(1, 1, 2, cells)


def solution(mesh):
    return jax.shard_map(
        per_device,
        mesh=mesh,
        in_specs=(P("ka", "ba", None, None), P()),
        out_specs=P("ka", "ba", None, None),
        check_vma=False,
    )
```

```python
import math

import jax
import jax.numpy as jnp
from jax import lax
from jax.experimental import pallas as pl
from jax.experimental.pallas import tpu as pltpu
from jax.sharding import PartitionSpec as P

LANES = 128


class Layout:
    def __init__(self, cells):
        self.grid = round(cells ** (1.0 / 3.0))
        self.low = LANES // self.grid
        self.high = self.grid // self.low
        self.rows = self.grid * self.high


def cosine(steps, grid):
    folded = jnp.abs((steps & (grid - 1)) - grid // 2) - grid // 4
    angle = folded.astype(jnp.float32) * (2.0 * math.pi / grid)
    square = angle * angle
    series = jnp.zeros_like(angle)
    for order in range(13, 1, -2):
        series = (series + (-1) ** (order // 2) / math.factorial(order)) * square
    return angle + angle * series


def sine(steps, grid):
    return cosine(steps - grid // 4, grid)


def setup_kernel(lay, by, coords_ref, rows_ref, forward_ref, inverse_ref, twiddle_ref, coulomb_ref):
    grid, high, rows = lay.grid, lay.high, lay.rows
    column = lax.broadcasted_iota(jnp.int32, (rows, 1), 0)
    across = lax.broadcasted_iota(jnp.int32, (1, rows), 1)
    steps = (column // high) * (across // high) + lay.low * (column % high) * (across % high)
    rows_ref[:rows] = cosine(steps, grid).astype(jnp.bfloat16)
    rows_ref[rows:] = sine(steps, grid).astype(jnp.bfloat16)

    lane_row = lax.broadcasted_iota(jnp.int32, (LANES, 1), 0)
    lane = lax.broadcasted_iota(jnp.int32, (1, LANES), 1)
    steps = high * (lane_row // grid) * (lane // grid) + (lane_row % grid) * (lane % grid)
    cos = cosine(steps, grid).astype(jnp.bfloat16)
    sin = sine(steps, grid)
    minus = (-sin).astype(jnp.bfloat16)
    sin = sin.astype(jnp.bfloat16)
    for ref, lower, upper in ((forward_ref, sin, minus), (inverse_ref, minus, sin)):
        ref[:LANES, :LANES] = cos
        ref[LANES:, LANES:] = cos
        ref[LANES:, :LANES] = lower
        ref[:LANES, LANES:] = upper

    steps = (column % high) * (lane // grid)
    twiddle_ref[:rows] = cosine(steps, grid)
    twiddle_ref[rows:] = sine(steps, grid)

    kpoints = coords_ref.shape[1]
    here = worker(lax.axis_index("ka"), kpoints)
    there = lax.rem(here + kpoints - by, kpoints)
    offset = [(coords_ref[d, here] - coords_ref[d, there]).astype(jnp.float32) / 4.0 for d in range(3)]

    def signed(index):
        return jnp.where(index < grid // 2, index, index - grid).astype(jnp.float32)

    along_x = signed(column // high) + offset[0]
    along_y = signed(lane // grid * high + column % high) + offset[1]
    along_z = signed(lane % grid) + offset[2]
    square = along_x * along_x + along_y * along_y + along_z * along_z
    coulomb_ref[...] = 32.0 / grid**3 / (square + 0.25)


def interleaved(field, lay):
    return field.reshape(2, lay.rows, LANES).transpose(1, 0, 2).reshape(2 * lay.rows, LANES)


def parity(k, kpoints):
    return k % 2 if kpoints % 8 == 0 else 0 * k


def worker(k, kpoints):
    return k + 1 - 2 * parity(k, kpoints) if kpoints % 8 == 0 else k


def split_parts(ref, scratch, rows):
    scratch[...] = ref[...].astype(jnp.float32)
    return scratch[pl.ds(0, rows, 2), :], scratch[pl.ds(1, rows, 2), :]


def exchange_kernel(rows, slots, *refs):
    matches = len(slots[0]) - 1
    target_refs, source_ref, refs = refs[:matches], refs[matches], refs[matches + 1 :]
    rows_ref, forward_ref, inverse_ref, twiddle_ref, coulomb_ref = refs[:5]
    out_refs, scratch = refs[5 : 6 + matches], refs[6 + matches :]
    kpoints = lax.axis_size("ka")
    odd = parity(worker(lax.axis_index("ka"), kpoints), kpoints) == 1
    f32, bf16 = jnp.float32, jnp.bfloat16

    def dot(a, b):
        return jnp.dot(a, b, preferred_element_type=f32)

    s_real, s_imag = split_parts(source_ref, scratch[0], rows)
    targets = [split_parts(target_refs[j], scratch[1 + j], rows) for j in range(matches)]
    coulomb = coulomb_ref[...]
    coulomb = jnp.concatenate([coulomb, coulomb], axis=1)

    pairs = []
    for t_real, t_imag in targets:
        real = s_real * t_real + s_imag * t_imag
        imag = s_real * t_imag - s_imag * t_real
        pairs.append(jnp.concatenate([real.astype(bf16), imag.astype(bf16)], axis=1))

    def turned(real, imag, cos, sin):
        return jnp.concatenate([(real * cos + imag * sin).astype(bf16), (imag * cos - real * sin).astype(bf16)], axis=1)

    row_cos, row_sin = rows_ref[:rows], rows_ref[rows:]
    tw_cos, tw_sin = twiddle_ref[:rows], twiddle_ref[rows:]
    both = [(dot(row_cos, pair), dot(row_sin, pair)) for pair in pairs]
    stage = [turned(c[:, :LANES] + s[:, LANES:], c[:, LANES:] - s[:, :LANES], tw_cos, tw_sin) for c, s in both]
    stage = [dot(field, forward_ref[...]) for field in stage]
    stage = [(field * coulomb).astype(bf16) for field in stage]
    stage = [dot(field, inverse_ref[...]) for field in stage]
    stage = [turned(field[:, :LANES], field[:, LANES:], tw_cos, -tw_sin) for field in stage]
    results = []
    total_real, total_imag = None, None
    for (t_real, t_imag), field in zip(targets, stage):
        c, s = dot(row_cos, field), dot(row_sin, field)
        v_real = c[:, :LANES] - s[:, LANES:]
        v_imag = c[:, LANES:] + s[:, :LANES]
        real = s_imag * v_imag - s_real * v_real
        imag = -(s_real * v_imag + s_imag * v_real)
        results.append((real.astype(bf16), imag.astype(bf16)))
        real = t_real * v_real + t_imag * v_imag
        imag = t_real * v_imag - t_imag * v_real
        total_real = real if total_real is None else total_real + real
        total_imag = imag if total_imag is None else total_imag + imag
    results.append(((-total_real).astype(bf16), total_imag.astype(bf16)))
    for out_ref, even_slot, odd_slot in zip(out_refs, *slots):
        for part, span in enumerate((slice(0, rows), slice(rows, 2 * rows))):
            value = results[even_slot][part]
            if even_slot != odd_slot:
                value = jnp.where(odd, results[odd_slot][part], value)
            out_ref[span] = value


def sum_kernel(rows, *refs):
    out_ref = refs[-1]
    total = refs[0][...].astype(jnp.float32)
    for ref in refs[1:-1]:
        total = total + ref[...].astype(jnp.float32)
    out_ref[pl.ds(0, rows, 2), :] = total[:rows]
    out_ref[pl.ds(1, rows, 2), :] = total[rows:]


def in_vmem(count):
    return [pl.BlockSpec(memory_space=pltpu.VMEM)] * count


def per_device(orbitals, kpoint_coords):
    own = orbitals[0, 0]
    cells = own.shape[-1]
    lay = Layout(cells)
    rows = lay.rows
    kpoints, groups = lax.axis_size("ka"), lax.axis_size("ba")
    steps = kpoints // 4
    matches = min(3, groups // 4 + 1)

    def moved(value, step, order, back):
        pairs = []
        for k in range(kpoints):
            for b in range(groups):
                part = order[parity(k, kpoints)][step]
                if part == matches:
                    home = (k - steps) % kpoints * groups + b
                else:
                    home = k * groups + (b ^ 2 ** ((part + parity(k, kpoints)) % matches))
                away = worker(k, kpoints) * groups + b
                pairs.append((away, home) if back else (home, away))
        return lax.ppermute(value, ("ka", "ba"), pairs)

    straight = list(range(matches + 1))
    arrivals = [moved(own, step, (straight, straight), False) for step in straight]
    slots = (straight[:matches][::-1] + straight[matches:], straight[matches:] + straight[:matches])

    def shape(*dims, dtype=jnp.bfloat16):
        return jax.ShapeDtypeStruct(dims, dtype)

    limits = pltpu.CompilerParams(vmem_limit_bytes=32 * 1024 * 1024)
    tables = pl.pallas_call(
        lambda *refs: setup_kernel(lay, steps, *refs),
        out_shape=[
            shape(2 * rows, rows),
            shape(2 * LANES, 2 * LANES),
            shape(2 * LANES, 2 * LANES),
            shape(2 * rows, LANES, dtype=jnp.float32),
            shape(rows, LANES, dtype=jnp.float32),
        ],
        in_specs=[pl.BlockSpec(memory_space=pltpu.SMEM)],
        out_specs=in_vmem(5),
        compiler_params=limits,
        name="setup",
    )(kpoint_coords.T)

    outs = pl.pallas_call(
        lambda *refs: exchange_kernel(rows, slots, *refs),
        out_shape=[shape(2 * rows, LANES)] * (matches + 1),
        in_specs=in_vmem(matches + 6),
        out_specs=in_vmem(matches + 1),
        scratch_shapes=[pltpu.VMEM((2 * rows, LANES), jnp.float32)] * (matches + 1),
        compiler_params=limits,
        name="exchange",
    )(*[interleaved(arrival, lay) for arrival in arrivals], *tables)
    returned = [moved(outs[step], step, slots, True) for step in straight]
    total = pl.pallas_call(
        lambda *refs: sum_kernel(rows, *refs),
        out_shape=shape(2 * rows, LANES, dtype=jnp.float32),
        in_specs=in_vmem(matches + 1),
        out_specs=in_vmem(1)[0],
        compiler_params=limits,
        name="total",
    )(*returned)
    return total.reshape(rows, 2, LANES).transpose(1, 0, 2).reshape(1, 1, 2, cells)


def solution(mesh):
    return jax.shard_map(
        per_device,
        mesh=mesh,
        in_specs=(P("ka", "ba", None, None), P()),
        out_specs=P("ka", "ba", None, None),
        check_vma=False,
    )
```

```python
import math

import jax
import jax.numpy as jnp
from jax import lax
from jax.experimental import pallas as pl
from jax.experimental.pallas import tpu as pltpu
from jax.sharding import PartitionSpec as P

LANES = 128


class Layout:
    def __init__(self, cells):
        self.grid = round(cells ** (1.0 / 3.0))
        self.low = LANES // self.grid
        self.high = self.grid // self.low
        self.rows = self.grid * self.high


def cosine(steps, grid):
    folded = jnp.abs((steps & (grid - 1)) - grid // 2) - grid // 4
    angle = folded.astype(jnp.float32) * (2.0 * math.pi / grid)
    square = angle * angle
    series = jnp.zeros_like(angle)
    for order in range(13, 1, -2):
        series = (series + (-1) ** (order // 2) / math.factorial(order)) * square
    return angle + angle * series


def sine(steps, grid):
    return cosine(steps - grid // 4, grid)


def setup_kernel(lay, by, coords_ref, rows_ref, forward_ref, inverse_ref, twiddle_ref, coulomb_ref):
    grid, high, rows = lay.grid, lay.high, lay.rows
    column = lax.broadcasted_iota(jnp.int32, (rows, 1), 0)
    across = lax.broadcasted_iota(jnp.int32, (1, rows), 1)
    steps = (column // high) * (across // high) + lay.low * (column % high) * (across % high)
    rows_ref[:rows] = cosine(steps, grid).astype(jnp.bfloat16)
    rows_ref[rows:] = sine(steps, grid).astype(jnp.bfloat16)

    lane_row = lax.broadcasted_iota(jnp.int32, (LANES, 1), 0)
    lane = lax.broadcasted_iota(jnp.int32, (1, LANES), 1)
    steps = high * (lane_row // grid) * (lane // grid) + (lane_row % grid) * (lane % grid)
    cos = cosine(steps, grid).astype(jnp.bfloat16)
    sin = sine(steps, grid)
    minus = (-sin).astype(jnp.bfloat16)
    sin = sin.astype(jnp.bfloat16)
    for ref, lower, upper in ((forward_ref, sin, minus), (inverse_ref, minus, sin)):
        ref[:LANES, :LANES] = cos
        ref[LANES:, LANES:] = cos
        ref[LANES:, :LANES] = lower
        ref[:LANES, LANES:] = upper

    steps = (column % high) * (lane // grid)
    twiddle_ref[:rows] = cosine(steps, grid)
    twiddle_ref[rows:] = sine(steps, grid)

    kpoints = coords_ref.shape[1]
    here = worker(lax.axis_index("ka"), kpoints)
    there = lax.rem(here + kpoints - by, kpoints)
    offset = [(coords_ref[d, here] - coords_ref[d, there]).astype(jnp.float32) / 4.0 for d in range(3)]

    def signed(index):
        return jnp.where(index < grid // 2, index, index - grid).astype(jnp.float32)

    along_x = signed(column // high) + offset[0]
    along_y = signed(lane // grid * high + column % high) + offset[1]
    along_z = signed(lane % grid) + offset[2]
    square = along_x * along_x + along_y * along_y + along_z * along_z
    coulomb_ref[...] = 32.0 / grid**3 / (square + 0.25)


def interleaved(field, lay):
    return field.reshape(2, lay.rows, LANES).transpose(1, 0, 2).reshape(2 * lay.rows, LANES)


def parity(k, kpoints):
    return k % 2 if kpoints % 8 == 0 else 0 * k


def worker(k, kpoints):
    return k ^ (k // 2 != 0) if kpoints % 8 == 0 else k


def split_parts(ref, scratch, rows):
    scratch[...] = ref[...].astype(jnp.float32)
    return scratch[pl.ds(0, rows, 2), :], scratch[pl.ds(1, rows, 2), :]


def exchange_kernel(rows, slots, *refs):
    matches = len(slots[0]) - 1
    target_refs, source_ref, refs = refs[:matches], refs[matches], refs[matches + 1 :]
    rows_ref, forward_ref, inverse_ref, twiddle_ref, coulomb_ref = refs[:5]
    out_refs, scratch = refs[5 : 6 + matches], refs[6 + matches :]
    kpoints = lax.axis_size("ka")
    odd = parity(worker(lax.axis_index("ka"), kpoints), kpoints) == 1
    f32, bf16 = jnp.float32, jnp.bfloat16

    def dot(a, b):
        return jnp.dot(a, b, preferred_element_type=f32)

    s_real, s_imag = split_parts(source_ref, scratch[0], rows)
    targets = [split_parts(target_refs[j], scratch[1 + j], rows) for j in range(matches)]
    coulomb = coulomb_ref[...]
    coulomb = jnp.concatenate([coulomb, coulomb], axis=1)

    pairs = []
    for t_real, t_imag in targets:
        real = s_real * t_real + s_imag * t_imag
        imag = s_real * t_imag - s_imag * t_real
        pairs.append(jnp.concatenate([real.astype(bf16), imag.astype(bf16)], axis=1))

    def turned(real, imag, cos, sin):
        return jnp.concatenate([(real * cos + imag * sin).astype(bf16), (imag * cos - real * sin).astype(bf16)], axis=1)

    row_cos, row_sin = rows_ref[:rows], rows_ref[rows:]
    tw_cos, tw_sin = twiddle_ref[:rows], twiddle_ref[rows:]
    both = [(dot(row_cos, pair), dot(row_sin, pair)) for pair in pairs]
    stage = [turned(c[:, :LANES] + s[:, LANES:], c[:, LANES:] - s[:, :LANES], tw_cos, tw_sin) for c, s in both]
    stage = [dot(field, forward_ref[...]) for field in stage]
    stage = [(field * coulomb).astype(bf16) for field in stage]
    stage = [dot(field, inverse_ref[...]) for field in stage]
    stage = [turned(field[:, :LANES], field[:, LANES:], tw_cos, -tw_sin) for field in stage]
    results = []
    total_real, total_imag = None, None
    for (t_real, t_imag), field in zip(targets, stage):
        c, s = dot(row_cos, field), dot(row_sin, field)
        v_real = c[:, :LANES] - s[:, LANES:]
        v_imag = c[:, LANES:] + s[:, :LANES]
        real = s_imag * v_imag - s_real * v_real
        imag = -(s_real * v_imag + s_imag * v_real)
        results.append((real.astype(bf16), imag.astype(bf16)))
        real = t_real * v_real + t_imag * v_imag
        imag = t_real * v_imag - t_imag * v_real
        total_real = real if total_real is None else total_real + real
        total_imag = imag if total_imag is None else total_imag + imag
    results.append(((-total_real).astype(bf16), total_imag.astype(bf16)))
    for out_ref, even_slot, odd_slot in zip(out_refs, *slots):
        for part, span in enumerate((slice(0, rows), slice(rows, 2 * rows))):
            value = results[even_slot][part]
            if even_slot != odd_slot:
                value = jnp.where(odd, results[odd_slot][part], value)
            out_ref[span] = value


def sum_kernel(rows, *refs):
    out_ref = refs[-1]
    total = refs[0][...].astype(jnp.float32)
    for ref in refs[1:-1]:
        total = total + ref[...].astype(jnp.float32)
    out_ref[pl.ds(0, rows, 2), :] = total[:rows]
    out_ref[pl.ds(1, rows, 2), :] = total[rows:]


def in_vmem(count):
    return [pl.BlockSpec(memory_space=pltpu.VMEM)] * count


def per_device(orbitals, kpoint_coords):
    own = orbitals[0, 0]
    cells = own.shape[-1]
    lay = Layout(cells)
    rows = lay.rows
    kpoints, groups = lax.axis_size("ka"), lax.axis_size("ba")
    steps = kpoints // 4
    matches = min(3, groups // 4 + 1)

    def moved(value, step, order, back):
        pairs = []
        for k in range(kpoints):
            for b in range(groups):
                part = order[parity(k, kpoints)][step]
                if part == matches:
                    home = (k - steps) % kpoints * groups + b
                else:
                    home = k * groups + (b ^ 2 ** ((part + parity(k, kpoints)) % matches))
                away = worker(k, kpoints) * groups + b
                pairs.append((away, home) if back else (home, away))
        return lax.ppermute(value, ("ka", "ba"), pairs)

    straight = list(range(matches + 1))
    arrivals = [moved(own, step, (straight, straight), False) for step in straight]
    slots = (straight[:matches][::-1] + straight[matches:], straight[matches:] + straight[:matches])

    def shape(*dims, dtype=jnp.bfloat16):
        return jax.ShapeDtypeStruct(dims, dtype)

    limits = pltpu.CompilerParams(vmem_limit_bytes=32 * 1024 * 1024)
    tables = pl.pallas_call(
        lambda *refs: setup_kernel(lay, steps, *refs),
        out_shape=[
            shape(2 * rows, rows),
            shape(2 * LANES, 2 * LANES),
            shape(2 * LANES, 2 * LANES),
            shape(2 * rows, LANES, dtype=jnp.float32),
            shape(rows, LANES, dtype=jnp.float32),
        ],
        in_specs=[pl.BlockSpec(memory_space=pltpu.SMEM)],
        out_specs=in_vmem(5),
        compiler_params=limits,
        name="setup",
    )(kpoint_coords.T)

    outs = pl.pallas_call(
        lambda *refs: exchange_kernel(rows, slots, *refs),
        out_shape=[shape(2 * rows, LANES)] * (matches + 1),
        in_specs=in_vmem(matches + 6),
        out_specs=in_vmem(matches + 1),
        scratch_shapes=[pltpu.VMEM((2 * rows, LANES), jnp.float32)] * (matches + 1),
        compiler_params=limits,
        name="exchange",
    )(*[interleaved(arrival, lay) for arrival in arrivals], *tables)
    returned = [moved(outs[step], step, slots, True) for step in straight]
    total = pl.pallas_call(
        lambda *refs: sum_kernel(rows, *refs),
        out_shape=shape(2 * rows, LANES, dtype=jnp.float32),
        in_specs=in_vmem(matches + 1),
        out_specs=in_vmem(1)[0],
        compiler_params=limits,
        name="total",
    )(*returned)
    return total.reshape(rows, 2, LANES).transpose(1, 0, 2).reshape(1, 1, 2, cells)


def solution(mesh):
    return jax.shard_map(
        per_device,
        mesh=mesh,
        in_specs=(P("ka", "ba", None, None), P()),
        out_specs=P("ka", "ba", None, None),
        check_vma=False,
    )
```

```python
import math

import jax
import jax.numpy as jnp
from jax import lax
from jax.experimental import pallas as pl
from jax.experimental.pallas import tpu as pltpu
from jax.sharding import PartitionSpec as P

LANES = 128


class Layout:
    def __init__(self, cells):
        self.grid = round(cells ** (1.0 / 3.0))
        self.low = LANES // self.grid
        self.high = self.grid // self.low
        self.rows = self.grid * self.high


def cosine(steps, grid):
    folded = jnp.abs((steps & (grid - 1)) - grid // 2) - grid // 4
    angle = folded.astype(jnp.float32) * (2.0 * math.pi / grid)
    square = angle * angle
    series = jnp.zeros_like(angle)
    for order in range(13, 1, -2):
        series = (series + (-1) ** (order // 2) / math.factorial(order)) * square
    return angle + angle * series


def sine(steps, grid):
    return cosine(steps - grid // 4, grid)


def setup_kernel(lay, by, coords_ref, rows_ref, forward_ref, inverse_ref, twiddle_ref, coulomb_ref):
    grid, high, rows = lay.grid, lay.high, lay.rows
    column = lax.broadcasted_iota(jnp.int32, (rows, 1), 0)
    across = lax.broadcasted_iota(jnp.int32, (1, rows), 1)
    steps = (column // high) * (across // high) + lay.low * (column % high) * (across % high)
    rows_ref[:rows] = cosine(steps, grid).astype(jnp.bfloat16)
    rows_ref[rows:] = sine(steps, grid).astype(jnp.bfloat16)

    lane_row = lax.broadcasted_iota(jnp.int32, (LANES, 1), 0)
    lane = lax.broadcasted_iota(jnp.int32, (1, LANES), 1)
    steps = high * (lane_row // grid) * (lane // grid) + (lane_row % grid) * (lane % grid)
    cos = cosine(steps, grid).astype(jnp.bfloat16)
    sin = sine(steps, grid)
    minus = (-sin).astype(jnp.bfloat16)
    sin = sin.astype(jnp.bfloat16)
    for ref, lower, upper in ((forward_ref, sin, minus), (inverse_ref, minus, sin)):
        ref[:LANES, :LANES] = cos
        ref[LANES:, LANES:] = cos
        ref[LANES:, :LANES] = lower
        ref[:LANES, LANES:] = upper

    steps = (column % high) * (lane // grid)
    twiddle_ref[:rows] = cosine(steps, grid)
    twiddle_ref[rows:] = sine(steps, grid)

    kpoints = coords_ref.shape[1]
    here = worker(lax.axis_index("ka"), kpoints)
    there = lax.rem(here + kpoints - by, kpoints)
    offset = [(coords_ref[d, here] - coords_ref[d, there]).astype(jnp.float32) / 4.0 for d in range(3)]

    def signed(index):
        return jnp.where(index < grid // 2, index, index - grid).astype(jnp.float32)

    along_x = signed(column // high) + offset[0]
    along_y = signed(lane // grid * high + column % high) + offset[1]
    along_z = signed(lane % grid) + offset[2]
    square = along_x * along_x + along_y * along_y + along_z * along_z
    coulomb_ref[...] = 32.0 / grid**3 / (square + 0.25)


def interleaved(field, lay):
    return field.reshape(2, lay.rows, LANES).transpose(1, 0, 2).reshape(2 * lay.rows, LANES)


def parity(k, kpoints):
    return k % 2 if kpoints % 8 == 0 else 0 * k


def worker(k, kpoints):
    return k + 1 - 2 * parity(k, kpoints) if kpoints % 8 == 0 else k


def split_parts(ref, scratch, rows):
    scratch[...] = ref[...].astype(jnp.float32)
    return scratch[pl.ds(0, rows, 2), :], scratch[pl.ds(1, rows, 2), :]


def exchange_kernel(rows, slots, *refs):
    matches = len(slots[0]) - 1
    target_refs, source_ref, refs = refs[:matches], refs[matches], refs[matches + 1 :]
    rows_ref, forward_ref, inverse_ref, twiddle_ref, coulomb_ref = refs[:5]
    out_refs, scratch = refs[5 : 6 + matches], refs[6 + matches :]
    kpoints = lax.axis_size("ka")
    odd = parity(worker(lax.axis_index("ka"), kpoints), kpoints) == 1
    f32, bf16 = jnp.float32, jnp.bfloat16

    def dot(a, b):
        return jnp.dot(a, b, preferred_element_type=f32)

    s_real, s_imag = split_parts(source_ref, scratch[0], rows)
    targets = [split_parts(target_refs[j], scratch[1 + j], rows) for j in range(matches)]
    coulomb = coulomb_ref[...]
    coulomb = jnp.concatenate([coulomb, coulomb], axis=1)

    pairs = []
    for t_real, t_imag in targets:
        real = s_real * t_real + s_imag * t_imag
        imag = s_real * t_imag - s_imag * t_real
        pairs.append(jnp.concatenate([real.astype(bf16), imag.astype(bf16)], axis=1))

    def turned(real, imag, cos, sin):
        return jnp.concatenate([(real * cos + imag * sin).astype(bf16), (imag * cos - real * sin).astype(bf16)], axis=1)

    row_cos, row_sin = rows_ref[:rows], rows_ref[rows:]
    tw_cos, tw_sin = twiddle_ref[:rows], twiddle_ref[rows:]
    both = [(dot(row_cos, pair), dot(row_sin, pair)) for pair in pairs]
    stage = [turned(c[:, :LANES] + s[:, LANES:], c[:, LANES:] - s[:, :LANES], tw_cos, tw_sin) for c, s in both]
    stage = [dot(field, forward_ref[...]) for field in stage]
    stage = [(field * coulomb).astype(bf16) for field in stage]
    stage = [dot(field, inverse_ref[...]) for field in stage]
    stage = [turned(field[:, :LANES], field[:, LANES:], tw_cos, -tw_sin) for field in stage]
    results = []
    total_real, total_imag = None, None
    for (t_real, t_imag), field in zip(targets, stage):
        c, s = dot(row_cos, field), dot(row_sin, field)
        v_real = c[:, :LANES] - s[:, LANES:]
        v_imag = c[:, LANES:] + s[:, :LANES]
        real = s_imag * v_imag - s_real * v_real
        imag = -(s_real * v_imag + s_imag * v_real)
        results.append((real.astype(bf16), imag.astype(bf16)))
        real = t_real * v_real + t_imag * v_imag
        imag = t_real * v_imag - t_imag * v_real
        total_real = real if total_real is None else total_real + real
        total_imag = imag if total_imag is None else total_imag + imag
    results.append(((-total_real).astype(bf16), total_imag.astype(bf16)))
    for out_ref, even_slot, odd_slot in zip(out_refs, *slots):
        for part, span in enumerate((slice(0, rows), slice(rows, 2 * rows))):
            value = results[even_slot][part]
            if even_slot != odd_slot:
                value = jnp.where(odd, results[odd_slot][part], value)
            out_ref[span] = value


def sum_kernel(rows, *refs):
    in_refs, out_ref, total_ref, sems = refs[:-3], refs[-3], refs[-2], refs[-1]
    count = sems.shape[0]
    size = rows // count
    copies = []
    for piece in range(count):
        for part in range(2):
            here = slice(part * rows + piece * size, part * rows + (piece + 1) * size)
            total = in_refs[0][here].astype(jnp.float32)
            for ref in in_refs[1:]:
                total = total + ref[here].astype(jnp.float32)
            total_ref[pl.ds(2 * piece * size + part, size, 2), :] = total
        span = pl.ds(2 * piece * size, 2 * size)
        copies.append(pltpu.make_async_copy(total_ref.at[span], out_ref.at[span], sems.at[piece]))
        copies[-1].start()
    for copy in copies:
        copy.wait()


def in_vmem(count):
    return [pl.BlockSpec(memory_space=pltpu.VMEM)] * count


def per_device(orbitals, kpoint_coords):
    own = orbitals[0, 0]
    cells = own.shape[-1]
    lay = Layout(cells)
    rows = lay.rows
    kpoints, groups = lax.axis_size("ka"), lax.axis_size("ba")
    steps = kpoints // 4
    matches = min(3, groups // 4 + 1)

    def moved(value, step, order, back):
        pairs = []
        for k in range(kpoints):
            for b in range(groups):
                part = order[parity(k, kpoints)][step]
                if part == matches:
                    home = (k - steps) % kpoints * groups + b
                else:
                    home = k * groups + (b ^ 2 ** ((part + parity(k, kpoints)) % matches))
                away = worker(k, kpoints) * groups + b
                pairs.append((away, home) if back else (home, away))
        return lax.ppermute(value, ("ka", "ba"), pairs)

    straight = list(range(matches + 1))
    arrivals = [moved(own, step, (straight, straight), False) for step in straight]
    slots = (straight[:matches][::-1] + straight[matches:], straight[matches:] + straight[:matches])

    def shape(*dims, dtype=jnp.bfloat16):
        return jax.ShapeDtypeStruct(dims, dtype)

    limits = pltpu.CompilerParams(vmem_limit_bytes=32 * 1024 * 1024)
    tables = pl.pallas_call(
        lambda *refs: setup_kernel(lay, steps, *refs),
        out_shape=[
            shape(2 * rows, rows),
            shape(2 * LANES, 2 * LANES),
            shape(2 * LANES, 2 * LANES),
            shape(2 * rows, LANES, dtype=jnp.float32),
            shape(rows, LANES, dtype=jnp.float32),
        ],
        in_specs=[pl.BlockSpec(memory_space=pltpu.SMEM)],
        out_specs=in_vmem(5),
        compiler_params=limits,
        name="setup",
    )(kpoint_coords.T)

    outs = pl.pallas_call(
        lambda *refs: exchange_kernel(rows, slots, *refs),
        out_shape=[shape(2 * rows, LANES)] * (matches + 1),
        in_specs=in_vmem(matches + 6),
        out_specs=in_vmem(matches + 1),
        scratch_shapes=[pltpu.VMEM((2 * rows, LANES), jnp.float32)] * (matches + 1),
        compiler_params=limits,
        name="exchange",
    )(*[interleaved(arrival, lay) for arrival in arrivals], *tables)
    returned = [moved(outs[step], step, slots, True) for step in straight]
    total = pl.pallas_call(
        lambda *refs: sum_kernel(rows, *refs),
        out_shape=shape(2 * rows, LANES, dtype=jnp.float32),
        in_specs=in_vmem(matches + 1),
        out_specs=pl.BlockSpec(memory_space=pl.ANY),
        scratch_shapes=[pltpu.VMEM((2 * rows, LANES), jnp.float32), pltpu.SemaphoreType.DMA((4,))],
        compiler_params=limits,
        name="total",
    )(*returned)
    return total.reshape(rows, 2, LANES).transpose(1, 0, 2).reshape(1, 1, 2, cells)


def solution(mesh):
    return jax.shard_map(
        per_device,
        mesh=mesh,
        in_specs=(P("ka", "ba", None, None), P()),
        out_specs=P("ka", "ba", None, None),
        check_vma=False,
    )
```

```python
import math

import jax
import jax.numpy as jnp
from jax import lax
from jax.experimental import pallas as pl
from jax.experimental.pallas import tpu as pltpu
from jax.sharding import PartitionSpec as P

LANES = 128


class Layout:
    def __init__(self, cells):
        self.grid = round(cells ** (1.0 / 3.0))
        self.low = LANES // self.grid
        self.high = self.grid // self.low
        self.rows = self.grid * self.high


def cosine(steps, grid):
    folded = jnp.abs((steps & (grid - 1)) - grid // 2) - grid // 4
    angle = folded.astype(jnp.float32) * (2.0 * math.pi / grid)
    square = angle * angle
    series = jnp.zeros_like(angle)
    for order in range(13, 1, -2):
        series = (series + (-1) ** (order // 2) / math.factorial(order)) * square
    return angle + angle * series


def sine(steps, grid):
    return cosine(steps - grid // 4, grid)


def setup_kernel(lay, by, coords_ref, rows_ref, forward_ref, inverse_ref, twiddle_ref, coulomb_ref):
    grid, high, rows = lay.grid, lay.high, lay.rows
    column = lax.broadcasted_iota(jnp.int32, (rows, 1), 0)
    across = lax.broadcasted_iota(jnp.int32, (1, rows), 1)
    steps = (column // high) * (across // high) + lay.low * (column % high) * (across % high)
    rows_ref[:rows] = cosine(steps, grid).astype(jnp.bfloat16)
    rows_ref[rows:] = sine(steps, grid).astype(jnp.bfloat16)

    lane_row = lax.broadcasted_iota(jnp.int32, (LANES, 1), 0)
    lane = lax.broadcasted_iota(jnp.int32, (1, LANES), 1)
    steps = high * (lane_row // grid) * (lane // grid) + (lane_row % grid) * (lane % grid)
    cos = cosine(steps, grid).astype(jnp.bfloat16)
    sin = sine(steps, grid)
    minus = (-sin).astype(jnp.bfloat16)
    sin = sin.astype(jnp.bfloat16)
    for ref, lower, upper in ((forward_ref, sin, minus), (inverse_ref, minus, sin)):
        ref[:LANES, :LANES] = cos
        ref[LANES:, LANES:] = cos
        ref[LANES:, :LANES] = lower
        ref[:LANES, LANES:] = upper

    steps = (column % high) * (lane // grid)
    twiddle_ref[:rows] = cosine(steps, grid)
    twiddle_ref[rows:] = sine(steps, grid)

    kpoints = coords_ref.shape[1]
    here = worker(lax.axis_index("ka"), kpoints)
    there = lax.rem(here + kpoints - by, kpoints)
    offset = [(coords_ref[d, here] - coords_ref[d, there]).astype(jnp.float32) / 4.0 for d in range(3)]

    def signed(index):
        return jnp.where(index < grid // 2, index, index - grid).astype(jnp.float32)

    along_x = signed(column // high) + offset[0]
    along_y = signed(lane // grid * high + column % high) + offset[1]
    along_z = signed(lane % grid) + offset[2]
    square = along_x * along_x + along_y * along_y + along_z * along_z
    coulomb_ref[...] = 32.0 / grid**3 / (square + 0.25)


def interleaved(field, lay):
    return field.reshape(2, lay.rows, LANES).transpose(1, 0, 2).reshape(2 * lay.rows, LANES)


def parity(k, kpoints):
    return k % 2 if kpoints % 8 == 0 else 0 * k


def worker(k, kpoints):
    return k + 1 - 2 * parity(k, kpoints) if kpoints % 8 == 0 else k


def split_parts(ref, scratch, rows):
    scratch[...] = ref[...].astype(jnp.float32)
    return scratch[pl.ds(0, rows, 2), :], scratch[pl.ds(1, rows, 2), :]


def exchange_kernel(rows, slots, *refs):
    matches = len(slots[0]) - 1
    target_refs, source_ref, refs = refs[:matches], refs[matches], refs[matches + 1 :]
    rows_ref, forward_ref, inverse_ref, twiddle_ref, coulomb_ref = refs[:5]
    out_refs, scratch = refs[5 : 6 + matches], refs[6 + matches :]
    kpoints = lax.axis_size("ka")
    odd = parity(worker(lax.axis_index("ka"), kpoints), kpoints) == 1
    f32, bf16 = jnp.float32, jnp.bfloat16

    def dot(a, b):
        return jnp.dot(a, b, preferred_element_type=f32)

    s_real, s_imag = split_parts(source_ref, scratch[0], rows)
    targets = [split_parts(target_refs[j], scratch[1 + j], rows) for j in range(matches)]
    coulomb = coulomb_ref[...]
    coulomb = jnp.concatenate([coulomb, coulomb], axis=1)

    pairs = []
    for t_real, t_imag in targets:
        real = s_real * t_real + s_imag * t_imag
        imag = s_real * t_imag - s_imag * t_real
        pairs.append(jnp.concatenate([real.astype(bf16), imag.astype(bf16)], axis=1))

    def turned(real, imag, cos, sin):
        return jnp.concatenate([(real * cos + imag * sin).astype(bf16), (imag * cos - real * sin).astype(bf16)], axis=1)

    row_cos, row_sin = rows_ref[:rows], rows_ref[rows:]
    tw_cos, tw_sin = twiddle_ref[:rows], twiddle_ref[rows:]
    both = [(dot(row_cos, pair), dot(row_sin, pair)) for pair in pairs]
    stage = [turned(c[:, :LANES] + s[:, LANES:], c[:, LANES:] - s[:, :LANES], tw_cos, tw_sin) for c, s in both]
    stage = [dot(field, forward_ref[...]) for field in stage]
    stage = [(field * coulomb).astype(bf16) for field in stage]
    stage = [dot(field, inverse_ref[...]) for field in stage]
    stage = [turned(field[:, :LANES], field[:, LANES:], tw_cos, -tw_sin) for field in stage]
    results = []
    total_real, total_imag = None, None
    for (t_real, t_imag), field in zip(targets, stage):
        c, s = dot(row_cos, field), dot(row_sin, field)
        v_real = c[:, :LANES] - s[:, LANES:]
        v_imag = c[:, LANES:] + s[:, :LANES]
        real = s_imag * v_imag - s_real * v_real
        imag = -(s_real * v_imag + s_imag * v_real)
        results.append((real.astype(bf16), imag.astype(bf16)))
        real = t_real * v_real + t_imag * v_imag
        imag = t_real * v_imag - t_imag * v_real
        total_real = real if total_real is None else total_real + real
        total_imag = imag if total_imag is None else total_imag + imag
    results.append(((-total_real).astype(bf16), total_imag.astype(bf16)))
    for out_ref, even_slot, odd_slot in zip(out_refs, *slots):
        for part, span in enumerate((slice(0, rows), slice(rows, 2 * rows))):
            value = results[even_slot][part]
            if even_slot != odd_slot:
                value = jnp.where(odd, results[odd_slot][part], value)
            out_ref[span] = value


def sum_kernel(rows, *refs):
    out_ref = refs[-1]
    total = refs[0][...].astype(jnp.float32)
    for ref in refs[1:-1]:
        total = total + ref[...].astype(jnp.float32)
    out_ref[pl.ds(0, rows, 2), :] = total[:rows]
    out_ref[pl.ds(1, rows, 2), :] = total[rows:]


def in_vmem(count):
    return [pl.BlockSpec(memory_space=pltpu.VMEM)] * count


def per_device(orbitals, kpoint_coords):
    own = orbitals[0, 0]
    cells = own.shape[-1]
    lay = Layout(cells)
    rows = lay.rows
    kpoints, groups = lax.axis_size("ka"), lax.axis_size("ba")
    steps = kpoints // 4
    matches = min(3, groups // 4 + 1)

    def moved(value, step, order, back):
        pairs = []
        for k in range(kpoints):
            for b in range(groups):
                part = order[parity(k, kpoints)][step]
                if part == matches:
                    home = (k - steps) % kpoints * groups + b
                else:
                    home = k * groups + (b ^ 2 ** ((part + parity(k, kpoints)) % matches))
                away = worker(k, kpoints) * groups + b
                pairs.append((away, home) if back else (home, away))
        return lax.ppermute(value, ("ka", "ba"), pairs)

    straight = list(range(matches + 1))
    arrivals = [moved(own, step, (straight, straight), False) for step in straight]
    slots = (straight[1:] + straight[:1], straight[:matches][::-1] + straight[matches:])

    def shape(*dims, dtype=jnp.bfloat16):
        return jax.ShapeDtypeStruct(dims, dtype)

    limits = pltpu.CompilerParams(vmem_limit_bytes=32 * 1024 * 1024)
    tables = pl.pallas_call(
        lambda *refs: setup_kernel(lay, steps, *refs),
        out_shape=[
            shape(2 * rows, rows),
            shape(2 * LANES, 2 * LANES),
            shape(2 * LANES, 2 * LANES),
            shape(2 * rows, LANES, dtype=jnp.float32),
            shape(rows, LANES, dtype=jnp.float32),
        ],
        in_specs=[pl.BlockSpec(memory_space=pltpu.SMEM)],
        out_specs=in_vmem(5),
        compiler_params=limits,
        name="setup",
    )(kpoint_coords.T)

    outs = pl.pallas_call(
        lambda *refs: exchange_kernel(rows, slots, *refs),
        out_shape=[shape(2 * rows, LANES)] * (matches + 1),
        in_specs=in_vmem(matches + 6),
        out_specs=in_vmem(matches + 1),
        scratch_shapes=[pltpu.VMEM((2 * rows, LANES), jnp.float32)] * (matches + 1),
        compiler_params=limits,
        name="exchange",
    )(*[interleaved(arrival, lay) for arrival in arrivals], *tables)
    returned = [moved(outs[step], step, slots, True) for step in straight]
    total = pl.pallas_call(
        lambda *refs: sum_kernel(rows, *refs),
        out_shape=shape(2 * rows, LANES, dtype=jnp.float32),
        in_specs=in_vmem(matches + 1),
        out_specs=in_vmem(1)[0],
        compiler_params=limits,
        name="total",
    )(*returned)
    return total.reshape(rows, 2, LANES).transpose(1, 0, 2).reshape(1, 1, 2, cells)


def solution(mesh):
    return jax.shard_map(
        per_device,
        mesh=mesh,
        in_specs=(P("ka", "ba", None, None), P()),
        out_specs=P("ka", "ba", None, None),
        check_vma=False,
    )
```

```python
import math

import jax
import jax.numpy as jnp
from jax import lax
from jax.experimental import pallas as pl
from jax.experimental.pallas import tpu as pltpu
from jax.sharding import PartitionSpec as P

LANES = 128


class Layout:
    def __init__(self, cells):
        self.grid = round(cells ** (1.0 / 3.0))
        self.low = LANES // self.grid
        self.high = self.grid // self.low
        self.rows = self.grid * self.high


def cosine(steps, grid):
    folded = jnp.abs((steps & (grid - 1)) - grid // 2) - grid // 4
    angle = folded.astype(jnp.float32) * (2.0 * math.pi / grid)
    square = angle * angle
    series = jnp.zeros_like(angle)
    for order in range(13, 1, -2):
        series = (series + (-1) ** (order // 2) / math.factorial(order)) * square
    return angle + angle * series


def sine(steps, grid):
    return cosine(steps - grid // 4, grid)


def setup_kernel(lay, by, coords_ref, rows_ref, forward_ref, inverse_ref, twiddle_ref, coulomb_ref):
    grid, high, rows = lay.grid, lay.high, lay.rows
    column = lax.broadcasted_iota(jnp.int32, (rows, 1), 0)
    across = lax.broadcasted_iota(jnp.int32, (1, rows), 1)
    steps = (column // high) * (across // high) + lay.low * (column % high) * (across % high)
    rows_ref[:rows] = cosine(steps, grid).astype(jnp.bfloat16)
    rows_ref[rows:] = sine(steps, grid).astype(jnp.bfloat16)

    lane_row = lax.broadcasted_iota(jnp.int32, (LANES, 1), 0)
    lane = lax.broadcasted_iota(jnp.int32, (1, LANES), 1)
    steps = high * (lane_row // grid) * (lane // grid) + (lane_row % grid) * (lane % grid)
    cos = cosine(steps, grid).astype(jnp.bfloat16)
    sin = sine(steps, grid)
    minus = (-sin).astype(jnp.bfloat16)
    sin = sin.astype(jnp.bfloat16)
    for ref, lower, upper in ((forward_ref, sin, minus), (inverse_ref, minus, sin)):
        ref[:LANES, :LANES] = cos
        ref[LANES:, LANES:] = cos
        ref[LANES:, :LANES] = lower
        ref[:LANES, LANES:] = upper

    steps = (column % high) * (lane // grid)
    twiddle_ref[:rows] = cosine(steps, grid)
    twiddle_ref[rows:] = sine(steps, grid)

    kpoints = coords_ref.shape[1]
    here = worker(lax.axis_index("ka"), kpoints)
    there = lax.rem(here + kpoints - by, kpoints)
    offset = [(coords_ref[d, here] - coords_ref[d, there]).astype(jnp.float32) / 4.0 for d in range(3)]

    def signed(index):
        return jnp.where(index < grid // 2, index, index - grid).astype(jnp.float32)

    along_x = signed(column // high) + offset[0]
    along_y = signed(lane // grid * high + column % high) + offset[1]
    along_z = signed(lane % grid) + offset[2]
    square = along_x * along_x + along_y * along_y + along_z * along_z
    coulomb_ref[...] = 32.0 / grid**3 / (square + 0.25)


def interleaved(field, lay):
    return field.reshape(2, lay.rows, LANES).transpose(1, 0, 2).reshape(2 * lay.rows, LANES)


def parity(k, kpoints):
    return k % 2 if kpoints % 8 == 0 else 0 * k


def worker(k, kpoints):
    return k + 1 - 2 * parity(k, kpoints) if kpoints % 8 == 0 else k


def split_parts(ref, scratch, rows):
    scratch[...] = ref[...].astype(jnp.float32)
    return scratch[pl.ds(0, rows, 2), :], scratch[pl.ds(1, rows, 2), :]


def exchange_kernel(rows, slots, *refs):
    matches = len(slots[0]) - 1
    target_refs, source_ref, refs = refs[:matches], refs[matches], refs[matches + 1 :]
    rows_ref, forward_ref, inverse_ref, twiddle_ref, coulomb_ref = refs[:5]
    out_refs, scratch = refs[5 : 6 + matches], refs[6 + matches :]
    kpoints = lax.axis_size("ka")
    odd = parity(worker(lax.axis_index("ka"), kpoints), kpoints) == 1
    f32, bf16 = jnp.float32, jnp.bfloat16

    def dot(a, b):
        return jnp.dot(a, b, preferred_element_type=f32)

    s_real, s_imag = split_parts(source_ref, scratch[0], rows)
    targets = [split_parts(target_refs[j], scratch[1 + j], rows) for j in range(matches)]
    coulomb = coulomb_ref[...]
    coulomb = jnp.concatenate([coulomb, coulomb], axis=1)

    pairs = []
    for t_real, t_imag in targets:
        real = s_real * t_real + s_imag * t_imag
        imag = s_real * t_imag - s_imag * t_real
        pairs.append(jnp.concatenate([real.astype(bf16), imag.astype(bf16)], axis=1))

    def turned(real, imag, cos, sin):
        return jnp.concatenate([(real * cos + imag * sin).astype(bf16), (imag * cos - real * sin).astype(bf16)], axis=1)

    row_cos, row_sin = rows_ref[:rows], rows_ref[rows:]
    tw_cos, tw_sin = twiddle_ref[:rows], twiddle_ref[rows:]
    both = [(dot(row_cos, pair), dot(row_sin, pair)) for pair in pairs]
    stage = [turned(c[:, :LANES] + s[:, LANES:], c[:, LANES:] - s[:, :LANES], tw_cos, tw_sin) for c, s in both]
    stacked = dot(jnp.concatenate(stage, axis=0), forward_ref[...])
    stacked = (stacked * jnp.concatenate([coulomb] * matches, axis=0)).astype(bf16)
    stacked = dot(stacked, inverse_ref[...])
    stage = [stacked[j * rows : (j + 1) * rows] for j in range(matches)]
    stage = [turned(field[:, :LANES], field[:, LANES:], tw_cos, -tw_sin) for field in stage]
    results = []
    total_real, total_imag = None, None
    for (t_real, t_imag), field in zip(targets, stage):
        c, s = dot(row_cos, field), dot(row_sin, field)
        v_real = c[:, :LANES] - s[:, LANES:]
        v_imag = c[:, LANES:] + s[:, :LANES]
        real = s_imag * v_imag - s_real * v_real
        imag = -(s_real * v_imag + s_imag * v_real)
        results.append((real.astype(bf16), imag.astype(bf16)))
        real = t_real * v_real + t_imag * v_imag
        imag = t_real * v_imag - t_imag * v_real
        total_real = real if total_real is None else total_real + real
        total_imag = imag if total_imag is None else total_imag + imag
    results.append(((-total_real).astype(bf16), total_imag.astype(bf16)))
    for out_ref, even_slot, odd_slot in zip(out_refs, *slots):
        for part, span in enumerate((slice(0, rows), slice(rows, 2 * rows))):
            value = results[even_slot][part]
            if even_slot != odd_slot:
                value = jnp.where(odd, results[odd_slot][part], value)
            out_ref[span] = value


def sum_kernel(rows, *refs):
    out_ref = refs[-1]
    total = refs[0][...].astype(jnp.float32)
    for ref in refs[1:-1]:
        total = total + ref[...].astype(jnp.float32)
    out_ref[pl.ds(0, rows, 2), :] = total[:rows]
    out_ref[pl.ds(1, rows, 2), :] = total[rows:]


def in_vmem(count):
    return [pl.BlockSpec(memory_space=pltpu.VMEM)] * count


def per_device(orbitals, kpoint_coords):
    own = orbitals[0, 0]
    cells = own.shape[-1]
    lay = Layout(cells)
    rows = lay.rows
    kpoints, groups = lax.axis_size("ka"), lax.axis_size("ba")
    steps = kpoints // 4
    matches = min(3, groups // 4 + 1)

    def moved(value, step, order, back):
        pairs = []
        for k in range(kpoints):
            for b in range(groups):
                part = order[parity(k, kpoints)][step]
                if part == matches:
                    home = (k - steps) % kpoints * groups + b
                else:
                    home = k * groups + (b ^ 2 ** ((part + parity(k, kpoints)) % matches))
                away = worker(k, kpoints) * groups + b
                pairs.append((away, home) if back else (home, away))
        return lax.ppermute(value, ("ka", "ba"), pairs)

    straight = list(range(matches + 1))
    arrivals = [moved(own, step, (straight, straight), False) for step in straight]
    slots = (straight[1:] + straight[:1], straight[:matches][::-1] + straight[matches:])

    def shape(*dims, dtype=jnp.bfloat16):
        return jax.ShapeDtypeStruct(dims, dtype)

    limits = pltpu.CompilerParams(vmem_limit_bytes=32 * 1024 * 1024)
    tables = pl.pallas_call(
        lambda *refs: setup_kernel(lay, steps, *refs),
        out_shape=[
            shape(2 * rows, rows),
            shape(2 * LANES, 2 * LANES),
            shape(2 * LANES, 2 * LANES),
            shape(2 * rows, LANES, dtype=jnp.float32),
            shape(rows, LANES, dtype=jnp.float32),
        ],
        in_specs=[pl.BlockSpec(memory_space=pltpu.SMEM)],
        out_specs=in_vmem(5),
        compiler_params=limits,
        name="setup",
    )(kpoint_coords.T)

    outs = pl.pallas_call(
        lambda *refs: exchange_kernel(rows, slots, *refs),
        out_shape=[shape(2 * rows, LANES)] * (matches + 1),
        in_specs=in_vmem(matches + 6),
        out_specs=in_vmem(matches + 1),
        scratch_shapes=[pltpu.VMEM((2 * rows, LANES), jnp.float32)] * (matches + 1),
        compiler_params=limits,
        name="exchange",
    )(*[interleaved(arrival, lay) for arrival in arrivals], *tables)
    returned = [moved(outs[step], step, slots, True) for step in straight]
    total = pl.pallas_call(
        lambda *refs: sum_kernel(rows, *refs),
        out_shape=shape(2 * rows, LANES, dtype=jnp.float32),
        in_specs=in_vmem(matches + 1),
        out_specs=in_vmem(1)[0],
        compiler_params=limits,
        name="total",
    )(*returned)
    return total.reshape(rows, 2, LANES).transpose(1, 0, 2).reshape(1, 1, 2, cells)


def solution(mesh):
    return jax.shard_map(
        per_device,
        mesh=mesh,
        in_specs=(P("ka", "ba", None, None), P()),
        out_specs=P("ka", "ba", None, None),
        check_vma=False,
    )
```

```python
import math

import jax
import jax.numpy as jnp
from jax import lax
from jax.experimental import pallas as pl
from jax.experimental.pallas import tpu as pltpu
from jax.sharding import PartitionSpec as P

LANES = 128


class Layout:
    def __init__(self, cells):
        self.grid = round(cells ** (1.0 / 3.0))
        self.low = LANES // self.grid
        self.high = self.grid // self.low
        self.rows = self.grid * self.high


def cosine(steps, grid):
    folded = jnp.abs((steps & (grid - 1)) - grid // 2) - grid // 4
    angle = folded.astype(jnp.float32) * (2.0 * math.pi / grid)
    square = angle * angle
    series = jnp.zeros_like(angle)
    for order in range(13, 1, -2):
        series = (series + (-1) ** (order // 2) / math.factorial(order)) * square
    return angle + angle * series


def sine(steps, grid):
    return cosine(steps - grid // 4, grid)


def setup_kernel(lay, by, coords_ref, rows_ref, forward_ref, inverse_ref, twiddle_ref, coulomb_ref):
    grid, high, rows = lay.grid, lay.high, lay.rows
    column = lax.broadcasted_iota(jnp.int32, (rows, 1), 0)
    across = lax.broadcasted_iota(jnp.int32, (1, rows), 1)
    steps = (column // high) * (across // high) + lay.low * (column % high) * (across % high)
    rows_ref[:rows] = cosine(steps, grid).astype(jnp.bfloat16)
    rows_ref[rows:] = sine(steps, grid).astype(jnp.bfloat16)

    lane_row = lax.broadcasted_iota(jnp.int32, (LANES, 1), 0)
    lane = lax.broadcasted_iota(jnp.int32, (1, LANES), 1)
    steps = high * (lane_row // grid) * (lane // grid) + (lane_row % grid) * (lane % grid)
    cos = cosine(steps, grid).astype(jnp.bfloat16)
    sin = sine(steps, grid)
    minus = (-sin).astype(jnp.bfloat16)
    sin = sin.astype(jnp.bfloat16)
    for ref, lower, upper in ((forward_ref, sin, minus), (inverse_ref, minus, sin)):
        ref[:LANES, :LANES] = cos
        ref[LANES:, LANES:] = cos
        ref[LANES:, :LANES] = lower
        ref[:LANES, LANES:] = upper

    steps = (column % high) * (lane // grid)
    twiddle_ref[:rows] = cosine(steps, grid)
    twiddle_ref[rows:] = sine(steps, grid)

    kpoints = coords_ref.shape[1]
    here = worker(lax.axis_index("ka"), kpoints)
    there = lax.rem(here + kpoints - by, kpoints)
    offset = [(coords_ref[d, here] - coords_ref[d, there]).astype(jnp.float32) / 4.0 for d in range(3)]

    def signed(index):
        return jnp.where(index < grid // 2, index, index - grid).astype(jnp.float32)

    along_x = signed(column // high) + offset[0]
    along_y = signed(lane // grid * high + column % high) + offset[1]
    along_z = signed(lane % grid) + offset[2]
    square = along_x * along_x + along_y * along_y + along_z * along_z
    coulomb_ref[...] = 32.0 / grid**3 / (square + 0.25)


def interleaved(field, lay):
    return field.reshape(2, lay.rows, LANES).transpose(1, 0, 2).reshape(2 * lay.rows, LANES)


def parity(k, kpoints):
    return k % 2 if kpoints % 8 == 0 else 0 * k


def worker(k, kpoints):
    return k + 1 - 2 * parity(k, kpoints) if kpoints % 8 == 0 else k


def split_parts(ref, scratch, rows):
    scratch[...] = ref[...].astype(jnp.float32)
    return scratch[pl.ds(0, rows, 2), :], scratch[pl.ds(1, rows, 2), :]


def early_kernel(rows, in_ref, out_ref, scratch):
    out_ref[:rows], out_ref[rows:] = split_parts(in_ref, scratch, rows)


def exchange_kernel(rows, slots, *refs):
    matches = len(slots[0]) - 1
    target_refs, source_ref, refs = refs[:matches], refs[matches], refs[matches + 1 :]
    rows_ref, forward_ref, inverse_ref, twiddle_ref, coulomb_ref = refs[:5]
    out_refs, scratch = refs[5 : 6 + matches], refs[6 + matches :]
    kpoints = lax.axis_size("ka")
    odd = parity(worker(lax.axis_index("ka"), kpoints), kpoints) == 1
    f32, bf16 = jnp.float32, jnp.bfloat16

    def dot(a, b):
        return jnp.dot(a, b, preferred_element_type=f32)

    fields = []
    for ref, space in zip([*target_refs, source_ref], scratch):
        ready = ref.dtype == f32
        fields.append((ref[:rows], ref[rows:]) if ready else split_parts(ref, space, rows))
    targets, (s_real, s_imag) = fields[:matches], fields[matches]
    coulomb = coulomb_ref[...]
    coulomb = jnp.concatenate([coulomb, coulomb], axis=1)

    pairs = []
    for t_real, t_imag in targets:
        real = s_real * t_real + s_imag * t_imag
        imag = s_real * t_imag - s_imag * t_real
        pairs.append(jnp.concatenate([real.astype(bf16), imag.astype(bf16)], axis=1))

    def turned(real, imag, cos, sin):
        return jnp.concatenate([(real * cos + imag * sin).astype(bf16), (imag * cos - real * sin).astype(bf16)], axis=1)

    row_cos, row_sin = rows_ref[:rows], rows_ref[rows:]
    tw_cos, tw_sin = twiddle_ref[:rows], twiddle_ref[rows:]
    both = [(dot(row_cos, pair), dot(row_sin, pair)) for pair in pairs]
    stage = [turned(c[:, :LANES] + s[:, LANES:], c[:, LANES:] - s[:, :LANES], tw_cos, tw_sin) for c, s in both]
    stage = [dot(field, forward_ref[...]) for field in stage]
    stage = [(field * coulomb).astype(bf16) for field in stage]
    stage = [dot(field, inverse_ref[...]) for field in stage]
    stage = [turned(field[:, :LANES], field[:, LANES:], tw_cos, -tw_sin) for field in stage]
    results = []
    total_real, total_imag = None, None
    for (t_real, t_imag), field in zip(targets, stage):
        c, s = dot(row_cos, field), dot(row_sin, field)
        v_real = c[:, :LANES] - s[:, LANES:]
        v_imag = c[:, LANES:] + s[:, :LANES]
        real = s_imag * v_imag - s_real * v_real
        imag = -(s_real * v_imag + s_imag * v_real)
        results.append((real.astype(bf16), imag.astype(bf16)))
        real = t_real * v_real + t_imag * v_imag
        imag = t_real * v_imag - t_imag * v_real
        total_real = real if total_real is None else total_real + real
        total_imag = imag if total_imag is None else total_imag + imag
    results.append(((-total_real).astype(bf16), total_imag.astype(bf16)))
    for out_ref, even_slot, odd_slot in zip(out_refs, *slots):
        for part, span in enumerate((slice(0, rows), slice(rows, 2 * rows))):
            value = results[even_slot][part]
            if even_slot != odd_slot:
                value = jnp.where(odd, results[odd_slot][part], value)
            out_ref[span] = value


def sum_kernel(rows, *refs):
    out_ref = refs[-1]
    total = refs[0][...].astype(jnp.float32)
    for ref in refs[1:-1]:
        total = total + ref[...].astype(jnp.float32)
    out_ref[pl.ds(0, rows, 2), :] = total[:rows]
    out_ref[pl.ds(1, rows, 2), :] = total[rows:]


def in_vmem(count):
    return [pl.BlockSpec(memory_space=pltpu.VMEM)] * count


def per_device(orbitals, kpoint_coords):
    own = orbitals[0, 0]
    cells = own.shape[-1]
    lay = Layout(cells)
    rows = lay.rows
    kpoints, groups = lax.axis_size("ka"), lax.axis_size("ba")
    steps = kpoints // 4
    matches = min(3, groups // 4 + 1)

    def moved(value, step, order, back):
        pairs = []
        for k in range(kpoints):
            for b in range(groups):
                part = order[parity(k, kpoints)][step]
                if part == matches:
                    home = (k - steps) % kpoints * groups + b
                else:
                    home = k * groups + (b ^ 2 ** ((part + parity(k, kpoints)) % matches))
                away = worker(k, kpoints) * groups + b
                pairs.append((away, home) if back else (home, away))
        return lax.ppermute(value, ("ka", "ba"), pairs)

    straight = list(range(matches + 1))
    arrivals = [moved(own, step, (straight, straight), False) for step in straight]
    slots = (straight[:matches][::-1] + straight[matches:], straight[matches:] + straight[:matches])

    def shape(*dims, dtype=jnp.bfloat16):
        return jax.ShapeDtypeStruct(dims, dtype)

    limits = pltpu.CompilerParams(vmem_limit_bytes=32 * 1024 * 1024)
    tables = pl.pallas_call(
        lambda *refs: setup_kernel(lay, steps, *refs),
        out_shape=[
            shape(2 * rows, rows),
            shape(2 * LANES, 2 * LANES),
            shape(2 * LANES, 2 * LANES),
            shape(2 * rows, LANES, dtype=jnp.float32),
            shape(rows, LANES, dtype=jnp.float32),
        ],
        in_specs=[pl.BlockSpec(memory_space=pltpu.SMEM)],
        out_specs=in_vmem(5),
        compiler_params=limits,
        name="setup",
    )(kpoint_coords.T)

    inputs = [interleaved(arrival, lay) for arrival in arrivals]
    for early in [matches]:
        inputs[early] = pl.pallas_call(
            lambda *refs: early_kernel(rows, *refs),
            out_shape=shape(2 * rows, LANES, dtype=jnp.float32),
            in_specs=in_vmem(1),
            out_specs=in_vmem(1)[0],
            scratch_shapes=[pltpu.VMEM((2 * rows, LANES), jnp.float32)],
            compiler_params=limits,
            name="early",
        )(inputs[early])
    outs = pl.pallas_call(
        lambda *refs: exchange_kernel(rows, slots, *refs),
        out_shape=[shape(2 * rows, LANES)] * (matches + 1),
        in_specs=in_vmem(matches + 6),
        out_specs=in_vmem(matches + 1),
        scratch_shapes=[pltpu.VMEM((2 * rows, LANES), jnp.float32)] * (matches + 1),
        compiler_params=limits,
        name="exchange",
    )(*inputs, *tables)
    returned = [moved(outs[step], step, slots, True) for step in straight]
    total = pl.pallas_call(
        lambda *refs: sum_kernel(rows, *refs),
        out_shape=shape(2 * rows, LANES, dtype=jnp.float32),
        in_specs=in_vmem(matches + 1),
        out_specs=in_vmem(1)[0],
        compiler_params=limits,
        name="total",
    )(*returned)
    return total.reshape(rows, 2, LANES).transpose(1, 0, 2).reshape(1, 1, 2, cells)


def solution(mesh):
    return jax.shard_map(
        per_device,
        mesh=mesh,
        in_specs=(P("ka", "ba", None, None), P()),
        out_specs=P("ka", "ba", None, None),
        check_vma=False,
    )
```

```python
import math

import jax
import jax.numpy as jnp
from jax import lax
from jax.experimental import pallas as pl
from jax.experimental.pallas import tpu as pltpu
from jax.sharding import PartitionSpec as P

LANES = 128


class Layout:
    def __init__(self, cells):
        self.grid = round(cells ** (1.0 / 3.0))
        self.low = LANES // self.grid
        self.high = self.grid // self.low
        self.rows = self.grid * self.high


def cosine(steps, grid):
    folded = jnp.abs((steps & (grid - 1)) - grid // 2) - grid // 4
    angle = folded.astype(jnp.float32) * (2.0 * math.pi / grid)
    square = angle * angle
    series = jnp.zeros_like(angle)
    for order in range(13, 1, -2):
        series = (series + (-1) ** (order // 2) / math.factorial(order)) * square
    return angle + angle * series


def sine(steps, grid):
    return cosine(steps - grid // 4, grid)


def setup_kernel(lay, by, coords_ref, rows_ref, forward_ref, inverse_ref, twiddle_ref, coulomb_ref):
    grid, high, rows = lay.grid, lay.high, lay.rows
    column = lax.broadcasted_iota(jnp.int32, (rows, 1), 0)
    across = lax.broadcasted_iota(jnp.int32, (1, rows), 1)
    steps = (column // high) * (across // high) + lay.low * (column % high) * (across % high)
    rows_ref[:rows] = cosine(steps, grid).astype(jnp.bfloat16)
    rows_ref[rows:] = sine(steps, grid).astype(jnp.bfloat16)

    lane_row = lax.broadcasted_iota(jnp.int32, (LANES, 1), 0)
    lane = lax.broadcasted_iota(jnp.int32, (1, LANES), 1)
    steps = high * (lane_row // grid) * (lane // grid) + (lane_row % grid) * (lane % grid)
    cos = cosine(steps, grid).astype(jnp.bfloat16)
    sin = sine(steps, grid)
    minus = (-sin).astype(jnp.bfloat16)
    sin = sin.astype(jnp.bfloat16)
    for ref, lower, upper in ((forward_ref, sin, minus), (inverse_ref, minus, sin)):
        ref[:LANES, :LANES] = cos
        ref[LANES:, LANES:] = cos
        ref[LANES:, :LANES] = lower
        ref[:LANES, LANES:] = upper

    steps = (column % high) * (lane // grid)
    twiddle_ref[:rows] = cosine(steps, grid)
    twiddle_ref[rows:] = sine(steps, grid)

    kpoints = coords_ref.shape[1]
    here = worker(lax.axis_index("ka"), kpoints)
    there = lax.rem(here + kpoints - by, kpoints)
    offset = [(coords_ref[d, here] - coords_ref[d, there]).astype(jnp.float32) / 4.0 for d in range(3)]

    def signed(index):
        return jnp.where(index < grid // 2, index, index - grid).astype(jnp.float32)

    along_x = signed(column // high) + offset[0]
    along_y = signed(lane // grid * high + column % high) + offset[1]
    along_z = signed(lane % grid) + offset[2]
    square = along_x * along_x + along_y * along_y + along_z * along_z
    coulomb_ref[...] = 32.0 / grid**3 / (square + 0.25)


def interleaved(field, lay):
    return field.reshape(2, lay.rows, LANES).transpose(1, 0, 2).reshape(2 * lay.rows, LANES)


def parity(k, kpoints):
    return k % 2 if kpoints % 8 == 0 else 0 * k


def worker(k, kpoints):
    return k + 1 - 2 * parity(k, kpoints) if kpoints % 8 == 0 else k


def split_parts(ref, scratch, rows):
    scratch[...] = ref[...].astype(jnp.float32)
    return scratch[pl.ds(0, rows, 2), :], scratch[pl.ds(1, rows, 2), :]


def exchange_kernel(rows, slots, *refs):
    matches = len(slots[0]) - 1
    target_refs, source_ref, refs = refs[:matches], refs[matches], refs[matches + 1 :]
    rows_ref, forward_ref, inverse_ref, twiddle_ref, coulomb_ref = refs[:5]
    out_refs, scratch = refs[5 : 6 + matches], refs[6 + matches :]
    kpoints = lax.axis_size("ka")
    odd = parity(worker(lax.axis_index("ka"), kpoints), kpoints) == 1
    f32, bf16 = jnp.float32, jnp.bfloat16

    def dot(a, b):
        return jnp.dot(a, b, preferred_element_type=f32)

    s_real, s_imag = split_parts(source_ref, scratch[0], rows)
    targets = [split_parts(target_refs[j], scratch[1 + j], rows) for j in range(matches)]
    coulomb = coulomb_ref[...]
    coulomb = jnp.concatenate([coulomb, coulomb], axis=1)

    pairs = []
    for t_real, t_imag in targets:
        real = s_real * t_real + s_imag * t_imag
        imag = s_real * t_imag - s_imag * t_real
        pairs.append(jnp.concatenate([real.astype(bf16), imag.astype(bf16)], axis=1))

    def turned(real, imag, cos, sin):
        return jnp.concatenate([(real * cos + imag * sin).astype(bf16), (imag * cos - real * sin).astype(bf16)], axis=1)

    row_cos, row_sin = rows_ref[:rows], rows_ref[rows:]
    tw_cos, tw_sin = twiddle_ref[:rows], twiddle_ref[rows:]
    both = [(dot(row_cos, pair), dot(row_sin, pair)) for pair in pairs]
    stage = [turned(c[:, :LANES] + s[:, LANES:], c[:, LANES:] - s[:, :LANES], tw_cos, tw_sin) for c, s in both]
    stage = [dot(field, forward_ref[...]) for field in stage]
    stage = [(field * coulomb).astype(bf16) for field in stage]
    stage = [dot(field, inverse_ref[...]) for field in stage]
    stage = [turned(field[:, :LANES], field[:, LANES:], tw_cos, -tw_sin) for field in stage]
    results = []
    total_real, total_imag = None, None
    for (t_real, t_imag), field in zip(targets, stage):
        c, s = dot(row_cos, field), dot(row_sin, field)
        v_real = c[:, :LANES] - s[:, LANES:]
        v_imag = c[:, LANES:] + s[:, :LANES]
        real = s_imag * v_imag - s_real * v_real
        imag = -(s_real * v_imag + s_imag * v_real)
        results.append((real.astype(bf16), imag.astype(bf16)))
        real = t_real * v_real + t_imag * v_imag
        imag = t_real * v_imag - t_imag * v_real
        total_real = real if total_real is None else total_real + real
        total_imag = imag if total_imag is None else total_imag + imag
    results.append(((-total_real).astype(bf16), total_imag.astype(bf16)))
    for out_ref, even_slot, odd_slot in zip(out_refs, *slots):
        for part, span in enumerate((slice(0, rows), slice(rows, 2 * rows))):
            value = results[even_slot][part]
            if even_slot != odd_slot:
                value = jnp.where(odd, results[odd_slot][part], value)
            out_ref[span] = value


def sum_kernel(rows, *refs):
    out_ref = refs[-1]
    total = refs[0][...].astype(jnp.float32)
    for ref in refs[1:-1]:
        total = total + ref[...].astype(jnp.float32)
    out_ref[pl.ds(0, rows, 2), :] = total[:rows]
    out_ref[pl.ds(1, rows, 2), :] = total[rows:]


def in_vmem(count):
    return [pl.BlockSpec(memory_space=pltpu.VMEM)] * count


def per_device(orbitals, kpoint_coords):
    own = orbitals[0, 0]
    cells = own.shape[-1]
    lay = Layout(cells)
    rows = lay.rows
    kpoints, groups = lax.axis_size("ka"), lax.axis_size("ba")
    steps = kpoints // 4
    matches = min(3, groups // 4 + 1)

    def moved(value, step, order, back):
        pairs = []
        for k in range(kpoints):
            for b in range(groups):
                part = order[parity(k, kpoints)][step]
                if part == matches:
                    home = (k - steps) % kpoints * groups + b
                else:
                    home = k * groups + (b ^ 2 ** ((part + parity(k, kpoints) + 1) % matches))
                away = worker(k, kpoints) * groups + b
                pairs.append((away, home) if back else (home, away))
        return lax.ppermute(value, ("ka", "ba"), pairs)

    straight = list(range(matches + 1))
    arrivals = [moved(own, step, (straight, straight), False) for step in straight]
    slots = (straight[1:] + straight[:1], straight[:matches][::-1] + straight[matches:])

    def shape(*dims, dtype=jnp.bfloat16):
        return jax.ShapeDtypeStruct(dims, dtype)

    limits = pltpu.CompilerParams(vmem_limit_bytes=32 * 1024 * 1024)
    tables = pl.pallas_call(
        lambda *refs: setup_kernel(lay, steps, *refs),
        out_shape=[
            shape(2 * rows, rows),
            shape(2 * LANES, 2 * LANES),
            shape(2 * LANES, 2 * LANES),
            shape(2 * rows, LANES, dtype=jnp.float32),
            shape(rows, LANES, dtype=jnp.float32),
        ],
        in_specs=[pl.BlockSpec(memory_space=pltpu.SMEM)],
        out_specs=in_vmem(5),
        compiler_params=limits,
        name="setup",
    )(kpoint_coords.T)

    outs = pl.pallas_call(
        lambda *refs: exchange_kernel(rows, slots, *refs),
        out_shape=[shape(2 * rows, LANES)] * (matches + 1),
        in_specs=in_vmem(matches + 6),
        out_specs=in_vmem(matches + 1),
        scratch_shapes=[pltpu.VMEM((2 * rows, LANES), jnp.float32)] * (matches + 1),
        compiler_params=limits,
        name="exchange",
    )(*[interleaved(arrival, lay) for arrival in arrivals], *tables)
    returned = [moved(outs[step], step, slots, True) for step in straight]
    total = pl.pallas_call(
        lambda *refs: sum_kernel(rows, *refs),
        out_shape=shape(2 * rows, LANES, dtype=jnp.float32),
        in_specs=in_vmem(matches + 1),
        out_specs=in_vmem(1)[0],
        compiler_params=limits,
        name="total",
    )(*returned)
    return total.reshape(rows, 2, LANES).transpose(1, 0, 2).reshape(1, 1, 2, cells)


def solution(mesh):
    return jax.shard_map(
        per_device,
        mesh=mesh,
        in_specs=(P("ka", "ba", None, None), P()),
        out_specs=P("ka", "ba", None, None),
        check_vma=False,
    )
```
